512 devices in a mesh: lat: 32 (over z_lo, x), lon: 8 (over y, z_hi), tp: 2 (over core).
Axes of the slice: x: 4, y: 4, z: 16 (z_hi: 2, z_lo: 8; z = z_hi * 8 + z_lo), core: 2. Of those that a mesh axis runs over, the one named last changes fastest.
Arguments:
- fine_tokens: bfloat16 [2, 384, 192, 512], P(None, 'lat', 'lon'), may hold values from -6 to 6
- attn_gain: float32 [512], replicated, may hold values from 0.1 to 1.9
- fine_qkv: bfloat16 [512, 3, 512], P('lat', None, 'tp'), may hold values from -4 to 4
- fine_proj: bfloat16 [512, 512], P(None, 'lat'), may hold values from -0.25 to 0.25
- merge_gain: float32 [2048], replicated, may hold values from 0.1 to 1.9
- merge_weight: bfloat16 [2048, 1024], P('lat', 'tp'), may hold values from -0.125 to 0.125
- coarse_gain: float32 [1024], replicated, may hold values from 0.1 to 1.9
- coarse_qkv: bfloat16 [1024, 3, 1024], P('lat', None, 'tp'), may hold values from -4 to 4
- coarse_proj: bfloat16 [1024, 1024], P('tp', 'lat'), may hold values from -0.1875 to 0.1875
- split_weight: bfloat16 [1024, 4, 512], P('lat', None, 'tp'), may hold values from -0.1875 to 0.1875
- split_gain: float32 [512], replicated, may hold values from 0.1 to 1.9
Outputs:
- restored: bfloat16 [2, 384, 192, 512], P(None, 'lat', 'lon', 'tp')
The draws below stay inside these ranges and needn't reach their ends.
All inputs are finite; a program needn't handle non-finite values.
Results may differ from the reference program's by a relative error of at most 0.013.
Values may be sent and summed in bfloat16 or wider, within the bound.
No kernel may reach another device: no remote copies, remote signals or barrier semaphores. Data moves between devices by JAX's collectives and lax.ppermute only.
A program may use at most 64 MiB of HBM per device.

```python
import jax
import jax.numpy as jnp
from jax import lax

D = 512
DC = 1024
HEAD = 64
FINE_HEADS = 8
COARSE_HEADS = 16
LEVELS = 2
WIN_LAT = 6
WIN_LON = 12
LAT_ALL = 384
LON_ALL = 192


def projection_base(key, fan_in, array_shape):
    base_values = jnp.clip(jax.random.normal(key, array_shape, jnp.float32), -4.0, 4.0)
    return base_values * fan_in ** (-0.5)


def draw_fine_qkv(key, part):
    key = jax.random.fold_in(key, 11)
    base_values = projection_base(key, D, (D, 3, FINE_HEADS * HEAD))
    return base_values.astype(jnp.bfloat16)


def draw_coarse_qkv(key, part):
    key = jax.random.fold_in(key, 23)
    base_values = projection_base(key, DC, (DC, 3, COARSE_HEADS * HEAD))
    return base_values.astype(jnp.bfloat16)


def block_scale(key, shape, pieces, least, high):
    loudness = 1.0
    for position, parts in pieces:
        heights = jax.random.uniform(jax.random.fold_in(jax.random.fold_in(key, 6), position), (parts,), jnp.float32, least / len(pieces), high / len(pieces))
        loudness = loudness * jnp.repeat(jnp.exp(heights), shape[position] // parts).reshape((-1,) + (1,) * (len(shape) - 1 - position))
    return loudness


def scatter_about(rng, extent, deviation, limit, cuts=(), kind=jnp.bfloat16):
    result = deviation * jax.random.normal(rng, extent, jnp.float32)
    if cuts:
        result = result * block_scale(rng, extent, cuts, -0.22, 0.18)
    return jnp.clip(result, -limit, limit).astype(kind)


def setup_inputs(seed: int = 0) -> dict:
    seeds = jax.random.split(jax.random.key(seed), 12)
    return {
        "fine_tokens": scatter_about(seeds[0], (LEVELS, LAT_ALL, LON_ALL, D), 1.0, 6.0, ((1, 32), (2, 8))),
        "attn_gain": jnp.clip(1.0 + 0.18 * jax.random.normal(seeds[1], (D,), jnp.float32), 0.1, 1.9),
        "fine_qkv": draw_fine_qkv(jax.random.fold_in(seeds[11], 71), 0),
        "fine_proj": scatter_about(seeds[3], (FINE_HEADS * HEAD, D), (FINE_HEADS * HEAD) ** -0.5, 0.25, ((1, 32),)),
        "merge_gain": jnp.clip(1.0 + 0.18 * jax.random.normal(seeds[4], (4 * D,), jnp.float32), 0.1, 1.9),
        "merge_weight": scatter_about(seeds[5], (4 * D, DC), (4 * D) ** -0.5, 0.125, ((0, 32), (1, 2))),
        "coarse_gain": jnp.clip(1.0 + 0.18 * jax.random.normal(seeds[6], (DC,), jnp.float32), 0.1, 1.9),
        "coarse_qkv": draw_coarse_qkv(jax.random.fold_in(seeds[11], 71), 0),
        "coarse_proj": scatter_about(seeds[8], (COARSE_HEADS * HEAD, DC), (COARSE_HEADS * HEAD) ** -0.5, 0.1875, ((0, 2), (1, 32))),
        "split_weight": scatter_about(seeds[9], (DC, 4, D), DC ** -0.5, 0.1875, ((0, 32), (2, 2))),
        "split_gain": jnp.clip(1.0 + 0.18 * jax.random.normal(seeds[10], (D,), jnp.float32), 0.1, 1.9),
    }


EPSILON = 1e-05

def layer_norm(values, gain_row):
    average = lax.optimization_barrier(jnp.mean(values, axis=-1, keepdims=True))
    centred = values - average
    spread = lax.optimization_barrier(jnp.mean(centred * centred, axis=-1, keepdims=True))
    return centred * lax.rsqrt(spread + EPSILON) * gain_row

def seam_labels(global_rows, lat_total, rim_rows):
    return jnp.where(global_rows >= lat_total - rim_rows, 1, jnp.where(global_rows < rim_rows, 2, 0)).astype(jnp.int32)

def window_mix(packed, head_count, row_labels):
    levels, row_count, col_count, channels = packed.shape
    head_size = channels // (3 * head_count)
    window_rows = row_count // WIN_LAT
    window_cols = col_count // WIN_LON
    window_size = levels * WIN_LAT * WIN_LON
    grouped = packed.reshape(levels, window_rows, WIN_LAT, window_cols, WIN_LON, 3, head_count, head_size)
    grouped = grouped.transpose(1, 3, 0, 2, 4, 5, 6, 7).reshape(window_rows * window_cols, window_size, 3, head_count, head_size)
    grouped = grouped.astype(jnp.float32)
    scores = jnp.einsum('wqhd,wkhd->whqk', grouped[:, :, 0], grouped[:, :, 1]) * head_size ** (-0.5)
    if row_labels is not None:
        token_labels = jnp.broadcast_to(row_labels.reshape(window_rows, 1, 1, WIN_LAT, 1), (window_rows, window_cols, levels, WIN_LAT, WIN_LON)).reshape(window_rows * window_cols, window_size)
        allowed = token_labels[:, :, None] == token_labels[:, None, :]
        scores = jnp.where(allowed[:, None], scores, -1e+30)
    row_maximum = lax.optimization_barrier(jnp.max(scores, axis=-1, keepdims=True))
    weights = jnp.exp(scores - row_maximum)
    weights = (weights / lax.optimization_barrier(jnp.sum(weights, axis=-1, keepdims=True))).astype(jnp.bfloat16)
    window_out = jnp.einsum('whqk,wkhd->wqhd', weights.astype(jnp.float32), grouped[:, :, 2]).astype(jnp.bfloat16)
    window_out = window_out.reshape(window_rows, window_cols, levels, WIN_LAT, WIN_LON, head_count * head_size).transpose(2, 0, 3, 1, 4, 5)
    return window_out.reshape(levels, row_count, col_count, head_count * head_size)

def reference(fine_tokens, attn_gain, fine_qkv, fine_proj, merge_gain, merge_weight, coarse_gain, coarse_qkv, coarse_proj, split_weight, split_gain):
    rim_rows = WIN_LAT // 2
    rim_cols = WIN_LON // 2
    rolled = jnp.roll(fine_tokens, (-rim_rows, -rim_cols), axis=(1, 2))
    band_count = LAT_ALL // WIN_LAT
    band_stack = rolled.reshape(LEVELS, band_count, WIN_LAT, LON_ALL, D).transpose(1, 0, 2, 3, 4)
    qkv_matrix = fine_qkv.reshape(D, 3 * FINE_HEADS * HEAD)

    def fine_band(inputs):
        band_rows, band_index = inputs
        flat_band = band_rows.reshape(-1, D)
        normed = layer_norm(flat_band.astype(jnp.float32), attn_gain).astype(jnp.bfloat16)
        packed = jnp.dot(normed, qkv_matrix, preferred_element_type=jnp.float32).astype(jnp.bfloat16)
        packed = packed.reshape(LEVELS, WIN_LAT, LON_ALL, 3 * FINE_HEADS * HEAD)
        global_rows = (band_index * WIN_LAT + rim_rows + jnp.arange(WIN_LAT, dtype=jnp.int32)) % LAT_ALL
        window_out = window_mix(packed, FINE_HEADS, seam_labels(global_rows, LAT_ALL, rim_rows))
        attended = jnp.dot(window_out.reshape(-1, FINE_HEADS * HEAD), fine_proj, preferred_element_type=jnp.float32)
        return (flat_band.astype(jnp.float32) + attended).astype(jnp.bfloat16).reshape(LEVELS, WIN_LAT, LON_ALL, D)
    finished = lax.map(fine_band, (band_stack, jnp.arange(band_count, dtype=jnp.int32)))
    residual = finished.transpose(1, 0, 2, 3, 4).reshape(LEVELS, LAT_ALL, LON_ALL, D)
    residual = jnp.roll(residual, (rim_rows, rim_cols), axis=(1, 2))
    pair_count = LAT_ALL // (2 * WIN_LAT)
    pair_stack = residual.reshape(LEVELS, pair_count, 2 * WIN_LAT, LON_ALL, D).transpose(1, 0, 2, 3, 4)
    half_cols = LON_ALL // 2

    def coarse_band(band_rows):
        quartets = band_rows.reshape(LEVELS, WIN_LAT, 2, half_cols, 2, D).transpose(0, 1, 3, 2, 4, 5).reshape(-1, 4 * D)
        merged_in = layer_norm(quartets.astype(jnp.float32), merge_gain).astype(jnp.bfloat16)
        coarse = jnp.dot(merged_in, merge_weight, preferred_element_type=jnp.float32).astype(jnp.bfloat16)
        coarse_normed = layer_norm(coarse.astype(jnp.float32), coarse_gain).astype(jnp.bfloat16)
        coarse_packed = jnp.dot(coarse_normed, coarse_qkv.reshape(DC, 3 * COARSE_HEADS * HEAD), preferred_element_type=jnp.float32).astype(jnp.bfloat16)
        coarse_packed = coarse_packed.reshape(LEVELS, WIN_LAT, half_cols, 3 * COARSE_HEADS * HEAD)
        coarse_mixed = window_mix(coarse_packed, COARSE_HEADS, None).reshape(-1, COARSE_HEADS * HEAD)
        update = jnp.dot(coarse_mixed, coarse_proj, preferred_element_type=jnp.float32)
        coarse_out = (coarse.astype(jnp.float32) + update).astype(jnp.bfloat16)
        expanded = jnp.dot(coarse_out, split_weight.reshape(DC, 4 * D), preferred_element_type=jnp.float32).reshape(-1, 4, D)
        first_sum = lax.optimization_barrier(jnp.sum(expanded, axis=-1))
        second_sum = lax.optimization_barrier(jnp.sum(expanded * expanded, axis=-1))
        average = first_sum / D
        spread = second_sum / D - average * average
        normed_split = (expanded - average[..., None]) * lax.rsqrt(spread[..., None] + EPSILON) * split_gain
        restored = normed_split.reshape(LEVELS, WIN_LAT, half_cols, 2, 2, D).transpose(0, 1, 3, 2, 4, 5).reshape(LEVELS, 2 * WIN_LAT, LON_ALL, D)
        return (band_rows.astype(jnp.float32) + restored).astype(jnp.bfloat16)
    outputs = lax.map(coarse_band, pair_stack)
    return outputs.transpose(1, 0, 2, 3, 4).reshape(LEVELS, LAT_ALL, LON_ALL, D)
```

```python
import jax
import jax.numpy as jnp
from jax import lax
from jax.sharding import Mesh, PartitionSpec as P

HEAD = 64
WIN_LAT = 6
WIN_LON = 12


EPSILON = 1e-05


def layer_norm(values, gain_row):
    average = jnp.mean(values, axis=-1, keepdims=True)
    centred = values - average
    spread = jnp.mean(centred * centred, axis=-1, keepdims=True)
    return centred * lax.rsqrt(spread + EPSILON) * gain_row


def seam_labels(global_rows, lat_total, rim_rows):
    return jnp.where(
        global_rows >= lat_total - rim_rows, 1, jnp.where(global_rows < rim_rows, 2, 0)
    ).astype(jnp.int32)


def window_mix(packed, head_count, row_labels):
    levels, row_count, col_count, channels = packed.shape
    head_size = channels // (3 * head_count)
    window_rows = row_count // WIN_LAT
    window_cols = col_count // WIN_LON
    window_size = levels * WIN_LAT * WIN_LON
    grouped = packed.reshape(
        levels, window_rows, WIN_LAT, window_cols, WIN_LON, 3, head_count, head_size
    )
    grouped = grouped.transpose(1, 3, 0, 2, 4, 5, 6, 7).reshape(
        window_rows * window_cols, window_size, 3, head_count, head_size
    )
    scores = jnp.einsum(
        "wqhd,wkhd->whqk", grouped[:, :, 0], grouped[:, :, 1], preferred_element_type=jnp.float32
    ) * head_size ** (-0.5)
    if row_labels is not None:
        token_labels = jnp.broadcast_to(
            row_labels.reshape(window_rows, 1, 1, WIN_LAT, 1),
            (window_rows, window_cols, levels, WIN_LAT, WIN_LON),
        ).reshape(window_rows * window_cols, window_size)
        allowed = token_labels[:, :, None] == token_labels[:, None, :]
        scores = jnp.where(allowed[:, None], scores, -1e30)
    row_maximum = jnp.max(scores, axis=-1, keepdims=True)
    weights = jnp.exp(scores - row_maximum)
    weights = (weights / jnp.sum(weights, axis=-1, keepdims=True)).astype(jnp.bfloat16)
    window_out = jnp.einsum(
        "whqk,wkhd->wqhd", weights, grouped[:, :, 2], preferred_element_type=jnp.float32
    ).astype(jnp.bfloat16)
    window_out = window_out.reshape(
        window_rows, window_cols, levels, WIN_LAT, WIN_LON, head_count * head_size
    ).transpose(2, 0, 3, 1, 4, 5)
    return window_out.reshape(levels, row_count, col_count, head_count * head_size)


def project_with(left_side, fragment):
    return jnp.dot(left_side, fragment, preferred_element_type=jnp.float32)


def project_with_transposed(left_side, fragment):
    return lax.dot_general(
        left_side, fragment, (((1,), (1,)), ((), ())), preferred_element_type=jnp.float32
    )


def quartered(shard, row_parts, col_parts):
    rows, cols = shard.shape[0] // row_parts, shard.shape[1] // col_parts
    place = lax.axis_index("y")
    return lax.dynamic_slice(
        shard, (place // col_parts * rows, place % col_parts * cols), (rows, cols)
    )


def sent_to_all(block, axes):
    peers = lax.axis_size(axes)
    copies = jnp.broadcast_to(block[None], (peers,) + block.shape)
    return lax.all_to_all(copies, axes, split_axis=0, concat_axis=0, tiled=True)


def over_depth(block):
    other = lax.ppermute(block, "za", [(0, 1), (1, 0)])
    upper = lax.axis_index("za") == 1
    pair = jnp.stack([jnp.where(upper, other, block), jnp.where(upper, block, other)])
    return sent_to_all(pair, "zq")


def over_plane(block, row_parts, col_parts):
    quads, pairs, rows, cols = block.shape
    whole = sent_to_all(block, ("x", "y"))
    whole = whole.reshape(4, row_parts, col_parts, quads, pairs, rows, cols)
    whole = whole.transpose(4, 3, 0, 1, 5, 2, 6)
    return whole.reshape(-1, col_parts * cols)


def after(value, earlier):
    return lax.optimization_barrier((value, earlier))[0]


def lat_shift(value, by):
    perm = [(i, (i + by) % 32) for i in range(32)]
    return lax.ppermute(value, ("za", "zq", "x"), perm)


def lon_shift(value, by):
    perm = [(i, (i + by) % 8) for i in range(8)]
    return lax.ppermute(value, ("y", "zh"), perm)


def body(
    fine_tokens,
    attn_gain,
    fine_qkv,
    fine_proj,
    merge_gain,
    merge_weight,
    coarse_gain,
    coarse_qkv,
    coarse_proj,
    split_weight,
    split_gain,
):
    levels, row_count, col_count, features = fine_tokens.shape
    lat_total = row_count * 32
    row_first = lax.axis_index(("za", "zq", "x")) * row_count
    rim_rows = WIN_LAT // 2
    rim_cols = WIN_LON // 2

    late_shard = jnp.concatenate([split_weight.reshape(32, -1), coarse_proj.T], axis=1)
    late = lax.all_gather(late_shard, "x", axis=0, tiled=True)
    late = lax.all_gather(late, ("za", "zq"), axis=0, tiled=True)
    packed_width = 3 * fine_qkv.shape[2]
    first_shard = jnp.concatenate([fine_qkv.reshape(16, packed_width), fine_proj.T], axis=1)
    first = over_depth(quartered(first_shard, 2, 2))
    first_all = over_plane(first, 2, 2)
    merge_depth = over_depth(after(quartered(merge_weight, 4, 1), first_all))
    qkv_depth = over_depth(after(quartered(coarse_qkv.reshape(32, -1), 4, 1), merge_depth))
    merge_all = over_plane(after(merge_depth, qkv_depth), 4, 1)
    qkv_all = over_plane(after(qkv_depth, merge_all), 4, 1)

    arriving = lon_shift(fine_tokens[:, :, :rim_cols], -1)
    extended = jnp.concatenate([fine_tokens[:, :, rim_cols:], arriving], axis=2)
    arriving = lat_shift(extended[:, :rim_rows], -1)
    extended = jnp.concatenate([extended[:, rim_rows:], arriving], axis=1)
    normed = layer_norm(extended.reshape(-1, features).astype(jnp.float32), attn_gain).astype(
        jnp.bfloat16
    )
    fine_heads = fine_qkv.shape[2] // HEAD
    packed = project_with(normed, first_all[:, :packed_width])
    packed = packed.astype(jnp.bfloat16).reshape(levels, row_count, col_count, packed_width)
    global_rows = (row_first + rim_rows + jnp.arange(row_count, dtype=jnp.int32)) % lat_total
    window_out = window_mix(packed, fine_heads, seam_labels(global_rows, lat_total, rim_rows))
    returning = lat_shift(window_out[:, row_count - rim_rows :], 1)
    window_out = jnp.concatenate([returning, window_out[:, : row_count - rim_rows]], axis=1)
    returning = lon_shift(window_out[:, :, col_count - rim_cols :], 1)
    window_out = jnp.concatenate([returning, window_out[:, :, : col_count - rim_cols]], axis=2)
    all_heads = lax.all_gather(window_out, "core", axis=3, tiled=True).reshape(-1, features)
    attended = project_with_transposed(all_heads, first_all[:, packed_width:])
    flat_tokens = fine_tokens.reshape(-1, features)
    residual = (flat_tokens.astype(jnp.float32) + attended).astype(jnp.bfloat16)
    half_rows = row_count // 2
    half_cols = col_count // 2
    quartets = (
        residual.reshape(levels, half_rows, 2, half_cols, 2, features)
        .transpose(0, 1, 3, 2, 4, 5)
        .reshape(-1, 4 * features)
    )
    merged_in = layer_norm(quartets.astype(jnp.float32), merge_gain).astype(jnp.bfloat16)
    coarse_rows = merged_in.shape[0]
    coarse_half = project_with(merged_in, merge_all).astype(jnp.bfloat16)
    coarse_full = lax.all_gather(coarse_half, "core", axis=1, tiled=True)
    coarse_normed = layer_norm(coarse_full.astype(jnp.float32), coarse_gain).astype(jnp.bfloat16)
    coarse_packed = project_with(coarse_normed, qkv_all).astype(jnp.bfloat16)
    heads_here = coarse_qkv.shape[2] // HEAD
    coarse_mixed = window_mix(
        coarse_packed.reshape(levels, half_rows, half_cols, -1), heads_here, None
    ).reshape(coarse_rows, -1)
    partial_value = project_with_transposed(coarse_mixed, late[:, 1024:]).astype(jnp.bfloat16)
    both = lax.all_gather(partial_value, "core", axis=0, tiled=False).astype(jnp.float32)
    coarse_out = (coarse_full.astype(jnp.float32) + (both[0] + both[1])).astype(jnp.bfloat16)
    feature_half = split_weight.shape[2]
    expanded = project_with(coarse_out, late[:, :1024])
    expanded = expanded.reshape(coarse_rows, 4, feature_half)
    first_sum, second_sum = lax.psum(
        (jnp.sum(expanded, axis=-1), jnp.sum(expanded * expanded, axis=-1)), "core"
    )
    average = first_sum / features
    spread = second_sum / features - average * average
    feature_start = lax.axis_index("core") * feature_half
    gain_part = lax.dynamic_slice_in_dim(split_gain, feature_start, feature_half, 0)
    normed_split = (
        (expanded - average[..., None]) * lax.rsqrt(spread[..., None] + EPSILON) * gain_part
    )
    restored = (
        normed_split.reshape(levels, half_rows, half_cols, 2, 2, feature_half)
        .transpose(0, 1, 3, 2, 4, 5)
        .reshape(levels, row_count, col_count, feature_half)
    )
    skip_part = lax.dynamic_slice_in_dim(
        residual.reshape(levels, row_count, col_count, features), feature_start, feature_half, 3
    )
    return (skip_part.astype(jnp.float32) + restored).astype(jnp.bfloat16)


def solution(mesh):
    finer = Mesh(
        mesh.devices.reshape(2, 4, 4, 4, 2, 2), ("za", "zq", "x", "y", "zh", "core")
    )
    lat, lon, tp = ("za", "zq", "x"), ("y", "zh"), "core"
    in_specs = (
        P(None, lat, lon, None),
        P(),
        P(lat, None, tp),
        P(None, lat),
        P(),
        P(lat, tp),
        P(),
        P(lat, None, tp),
        P(tp, lat),
        P(lat, None, tp),
        P(),
    )
    out_specs = P(None, lat, lon, tp)
    return jax.shard_map(body, mesh=finer, in_specs=in_specs, out_specs=out_specs, check_vma=False)
```

```python
import jax
import jax.numpy as jnp
from jax import lax
from jax.sharding import Mesh, PartitionSpec as P

HEAD = 64
WIN_LAT = 6
WIN_LON = 12


EPSILON = 1e-05


def layer_norm(values, gain_row):
    average = jnp.mean(values, axis=-1, keepdims=True)
    centred = values - average
    spread = jnp.mean(centred * centred, axis=-1, keepdims=True)
    return centred * lax.rsqrt(spread + EPSILON) * gain_row


def seam_labels(global_rows, lat_total, rim_rows):
    return jnp.where(
        global_rows >= lat_total - rim_rows, 1, jnp.where(global_rows < rim_rows, 2, 0)
    ).astype(jnp.int32)


def window_mix(packed, head_count, row_labels):
    levels, row_count, col_count, channels = packed.shape
    head_size = channels // (3 * head_count)
    window_rows = row_count // WIN_LAT
    window_cols = col_count // WIN_LON
    window_size = levels * WIN_LAT * WIN_LON
    grouped = packed.reshape(
        levels, window_rows, WIN_LAT, window_cols, WIN_LON, 3, head_count, head_size
    )
    grouped = grouped.transpose(1, 3, 0, 2, 4, 5, 6, 7).reshape(
        window_rows * window_cols, window_size, 3, head_count, head_size
    )
    scores = jnp.einsum(
        "wqhd,wkhd->whqk", grouped[:, :, 0], grouped[:, :, 1], preferred_element_type=jnp.float32
    ) * head_size ** (-0.5)
    if row_labels is not None:
        token_labels = jnp.broadcast_to(
            row_labels.reshape(window_rows, 1, 1, WIN_LAT, 1),
            (window_rows, window_cols, levels, WIN_LAT, WIN_LON),
        ).reshape(window_rows * window_cols, window_size)
        allowed = token_labels[:, :, None] == token_labels[:, None, :]
        scores = jnp.where(allowed[:, None], scores, -1e30)
    row_maximum = jnp.max(scores, axis=-1, keepdims=True)
    weights = jnp.exp(scores - row_maximum)
    weights = (weights / jnp.sum(weights, axis=-1, keepdims=True)).astype(jnp.bfloat16)
    window_out = jnp.einsum(
        "whqk,wkhd->wqhd", weights, grouped[:, :, 2], preferred_element_type=jnp.float32
    ).astype(jnp.bfloat16)
    window_out = window_out.reshape(
        window_rows, window_cols, levels, WIN_LAT, WIN_LON, head_count * head_size
    ).transpose(2, 0, 3, 1, 4, 5)
    return window_out.reshape(levels, row_count, col_count, head_count * head_size)


def project_with(left_side, fragment):
    return jnp.dot(left_side, fragment, preferred_element_type=jnp.float32)


def project_with_transposed(left_side, fragment):
    return lax.dot_general(
        left_side, fragment, (((1,), (1,)), ((), ())), preferred_element_type=jnp.float32
    )


def quartered(shard, row_parts, col_parts):
    rows, cols = shard.shape[0] // row_parts, shard.shape[1] // col_parts
    place = lax.axis_index("y")
    return lax.dynamic_slice(
        shard, (place // col_parts * rows, place % col_parts * cols), (rows, cols)
    )


def sent_to_all(block, axes):
    peers = lax.axis_size(axes)
    copies = jnp.broadcast_to(block[None], (peers,) + block.shape)
    return lax.all_to_all(copies, axes, split_axis=0, concat_axis=0, tiled=True)


def over_depth(block):
    other = lax.ppermute(block, "za", [(0, 1), (1, 0)])
    upper = lax.axis_index("za") == 1
    pair = jnp.stack([jnp.where(upper, other, block), jnp.where(upper, block, other)])
    return sent_to_all(pair, "zq")


def over_plane(block):
    return sent_to_all(block, ("x", "y")).reshape((4,) * 3 + block.shape[1:])


def after(value, earlier):
    return lax.optimization_barrier((value, earlier))[0]


def lat_shift(value, by):
    perm = [(i, (i + by) % 32) for i in range(32)]
    return lax.ppermute(value, ("za", "zq", "x"), perm)


def lon_shift(value, by):
    perm = [(i, (i + by) % 8) for i in range(8)]
    return lax.ppermute(value, ("y", "zh"), perm)


def body(
    fine_tokens,
    attn_gain,
    fine_qkv,
    fine_proj,
    merge_gain,
    merge_weight,
    coarse_gain,
    coarse_qkv,
    coarse_proj,
    split_weight,
    split_gain,
):
    levels, row_count, col_count, features = fine_tokens.shape
    lat_total = row_count * 32
    row_first = lax.axis_index(("za", "zq", "x")) * row_count
    rim_rows = WIN_LAT // 2
    rim_cols = WIN_LON // 2

    core = lax.axis_index("core")
    packed_width = 3 * fine_qkv.shape[2]
    first_shard = jnp.concatenate([fine_qkv.reshape(16, packed_width), fine_proj.T], axis=1)
    merge_part = quartered(merge_weight, 4, 1)
    depth = over_depth(
        jnp.concatenate(
            [
                quartered(first_shard, 2, 2),
                merge_part[:8],
                merge_part[8:],
                quartered(coarse_qkv.reshape(32, -1), 4, 1),
            ],
            axis=1,
        )
    )
    first_all = over_plane(depth[..., :640])
    merge_all = over_plane(after(depth[..., 640:1664], first_all))
    qkv_all = over_plane(after(depth[..., 1664:], merge_all))
    first_all = first_all.reshape(4, 2, 2, 4, 2, 8, 640)
    first_all = first_all.transpose(4, 3, 0, 1, 5, 2, 6).reshape(512, 1280)
    merge_all = merge_all.reshape(4, 4, 4, 2, 8, 2, 512)
    merge_all = merge_all.transpose(3, 2, 0, 1, 5, 4, 6).reshape(2048, 512)
    qkv_all = qkv_all.transpose(3, 2, 0, 1, 4, 5).reshape(1024, 1536)

    late_shard = jnp.concatenate([split_weight.reshape(32, -1), coarse_proj.T], axis=1)
    late = lax.all_gather(jnp.pad(late_shard, ((0, 56), (0, 0))), "x", axis=0, tiled=False)
    late = late[:, :32].reshape(128, 1536)
    late = lax.all_gather(late, ("za", "zq"), axis=0, tiled=True)

    own_half = lax.dynamic_slice_in_dim(
        after(fine_tokens, depth), core * (features // 2), features // 2, 3
    )
    east = lon_shift(own_half[:, :, :rim_cols], -1)
    west = lon_shift(own_half[:, :, col_count - rim_cols :], 1)
    strip = jnp.concatenate([west, own_half, east], axis=2)
    below = lat_shift(strip[:, :rim_rows], -1)
    above = lat_shift(strip[:, row_count - rim_rows :], 1)
    rims = [above, below, west, east]
    flat_rims = lax.all_gather(
        jnp.concatenate([rim.reshape(-1, features // 2) for rim in rims], axis=0),
        "core",
        axis=1,
        tiled=True,
    )
    whole, place = [], 0
    for rim in rims:
        rows = rim.size // (features // 2)
        whole.append(flat_rims[place : place + rows].reshape(rim.shape[:3] + (features,)))
        place += rows
    above, below, west, east = whole
    extended = jnp.concatenate(
        [above, jnp.concatenate([west, fine_tokens, east], axis=2), below], axis=1
    )
    wide_rows, wide_cols = extended.shape[1:3]
    normed = layer_norm(extended.reshape(-1, features).astype(jnp.float32), attn_gain).astype(
        jnp.bfloat16
    )
    fine_heads = fine_qkv.shape[2] // HEAD
    packed = project_with(normed, first_all[:, :packed_width])
    packed = packed.astype(jnp.bfloat16).reshape(levels, wide_rows, wide_cols, packed_width)
    global_rows = row_first - rim_rows + jnp.arange(wide_rows, dtype=jnp.int32)
    global_rows = (global_rows + lat_total) % lat_total
    window_out = window_mix(packed, fine_heads, seam_labels(global_rows, lat_total, rim_rows))
    window_out = window_out[
        :, rim_rows : rim_rows + row_count, rim_cols : rim_cols + col_count
    ]
    all_heads = lax.all_gather(window_out, "core", axis=3, tiled=True).reshape(-1, features)
    attended = project_with_transposed(all_heads, first_all[:, packed_width:])
    flat_tokens = fine_tokens.reshape(-1, features)
    residual = (flat_tokens.astype(jnp.float32) + attended).astype(jnp.bfloat16)
    half_rows = row_count // 2
    half_cols = col_count // 2
    quartets = (
        residual.reshape(levels, half_rows, 2, half_cols, 2, features)
        .transpose(0, 1, 3, 2, 4, 5)
        .reshape(-1, 4 * features)
    )
    merged_in = layer_norm(quartets.astype(jnp.float32), merge_gain).astype(jnp.bfloat16)
    coarse_rows = merged_in.shape[0]
    coarse_half = project_with(merged_in, merge_all).astype(jnp.bfloat16)
    coarse_full = lax.all_gather(coarse_half, "core", axis=1, tiled=True)
    coarse_normed = layer_norm(coarse_full.astype(jnp.float32), coarse_gain).astype(jnp.bfloat16)
    coarse_packed = project_with(coarse_normed, qkv_all).astype(jnp.bfloat16)
    heads_here = coarse_qkv.shape[2] // HEAD
    coarse_mixed = window_mix(
        coarse_packed.reshape(levels, half_rows, half_cols, -1), heads_here, None
    ).reshape(coarse_rows, -1)
    partial_value = project_with_transposed(coarse_mixed, late[:, 1024:]).astype(jnp.bfloat16)
    both = lax.all_gather(partial_value, "core", axis=0, tiled=False).astype(jnp.float32)
    coarse_out = (coarse_full.astype(jnp.float32) + (both[0] + both[1])).astype(jnp.bfloat16)
    feature_half = split_weight.shape[2]
    expanded = project_with(coarse_out, late[:, :1024])
    expanded = expanded.reshape(coarse_rows, 4, feature_half)
    first_sum, second_sum = lax.psum(
        (jnp.sum(expanded, axis=-1), jnp.sum(expanded * expanded, axis=-1)), "core"
    )
    average = first_sum / features
    spread = second_sum / features - average * average
    feature_start = core * feature_half
    gain_part = lax.dynamic_slice_in_dim(split_gain, feature_start, feature_half, 0)
    normed_split = (
        (expanded - average[..., None]) * lax.rsqrt(spread[..., None] + EPSILON) * gain_part
    )
    restored = (
        normed_split.reshape(levels, half_rows, half_cols, 2, 2, feature_half)
        .transpose(0, 1, 3, 2, 4, 5)
        .reshape(levels, row_count, col_count, feature_half)
    )
    skip_part = lax.dynamic_slice_in_dim(
        residual.reshape(levels, row_count, col_count, features), feature_start, feature_half, 3
    )
    return (skip_part.astype(jnp.float32) + restored).astype(jnp.bfloat16)


def solution(mesh):
    finer = Mesh(
        mesh.devices.reshape(2, 4, 4, 4, 2, 2), ("za", "zq", "x", "y", "zh", "core")
    )
    lat, lon, tp = ("za", "zq", "x"), ("y", "zh"), "core"
    in_specs = (
        P(None, lat, lon, None),
        P(),
        P(lat, None, tp),
        P(None, lat),
        P(),
        P(lat, tp),
        P(),
        P(lat, None, tp),
        P(tp, lat),
        P(lat, None, tp),
        P(),
    )
    out_specs = P(None, lat, lon, tp)
    return jax.shard_map(body, mesh=finer, in_specs=in_specs, out_specs=out_specs, check_vma=False)
```

```python
import jax
import jax.numpy as jnp
from jax import lax
from jax.experimental import pallas as pl
from jax.experimental.pallas import tpu as pltpu
from jax.sharding import Mesh, PartitionSpec as P

HEAD = 64
WIN_LAT = 6
WIN_LON = 12


EPSILON = 1e-05


def layer_norm(values, gain_row):
    average = jnp.mean(values, axis=-1, keepdims=True)
    centred = values - average
    spread = jnp.mean(centred * centred, axis=-1, keepdims=True)
    return centred * lax.rsqrt(spread + EPSILON) * gain_row


def seam_labels(global_rows, lat_total, rim_rows):
    return jnp.where(
        global_rows >= lat_total - rim_rows, 1, jnp.where(global_rows < rim_rows, 2, 0)
    ).astype(jnp.int32)


def window_mix(packed, head_count, row_labels):
    levels, row_count, col_count, channels = packed.shape
    head_size = channels // (3 * head_count)
    window_rows = row_count // WIN_LAT
    window_cols = col_count // WIN_LON
    window_size = levels * WIN_LAT * WIN_LON
    grouped = packed.reshape(
        levels, window_rows, WIN_LAT, window_cols, WIN_LON, 3, head_count, head_size
    )
    grouped = grouped.transpose(1, 3, 0, 2, 4, 5, 6, 7).reshape(
        window_rows * window_cols, window_size, 3, head_count, head_size
    )
    scores = jnp.einsum(
        "wqhd,wkhd->whqk", grouped[:, :, 0], grouped[:, :, 1], preferred_element_type=jnp.float32
    ) * head_size ** (-0.5)
    if row_labels is not None:
        token_labels = jnp.broadcast_to(
            row_labels.reshape(window_rows, 1, 1, WIN_LAT, 1),
            (window_rows, window_cols, levels, WIN_LAT, WIN_LON),
        ).reshape(window_rows * window_cols, window_size)
        allowed = token_labels[:, :, None] == token_labels[:, None, :]
        scores = jnp.where(allowed[:, None], scores, -1e30)
    row_maximum = jnp.max(scores, axis=-1, keepdims=True)
    weights = jnp.exp(scores - row_maximum)
    weights = (weights / jnp.sum(weights, axis=-1, keepdims=True)).astype(jnp.bfloat16)
    window_out = jnp.einsum(
        "whqk,wkhd->wqhd", weights, grouped[:, :, 2], preferred_element_type=jnp.float32
    ).astype(jnp.bfloat16)
    window_out = window_out.reshape(
        window_rows, window_cols, levels, WIN_LAT, WIN_LON, head_count * head_size
    ).transpose(2, 0, 3, 1, 4, 5)
    return window_out.reshape(levels, row_count, col_count, head_count * head_size)


def project_with(left_side, fragment):
    return jnp.dot(left_side, fragment, preferred_element_type=jnp.float32)


def project_with_transposed(left_side, fragment):
    return lax.dot_general(
        left_side, fragment, (((1,), (1,)), ((), ())), preferred_element_type=jnp.float32
    )


def quartered(shard, row_parts, col_parts):
    rows, cols = shard.shape[0] // row_parts, shard.shape[1] // col_parts
    place = lax.axis_index("y")
    return lax.dynamic_slice(
        shard, (place // col_parts * rows, place % col_parts * cols), (rows, cols)
    )


def sent_to_all(block, axes):
    peers = lax.axis_size(axes)
    copies = jnp.broadcast_to(block[None], (peers,) + block.shape)
    return lax.all_to_all(copies, axes, split_axis=0, concat_axis=0, tiled=True)


def over_depth(block):
    other = lax.ppermute(block, "za", [(0, 1), (1, 0)])
    upper = lax.axis_index("za") == 1
    pair = jnp.stack([jnp.where(upper, other, block), jnp.where(upper, block, other)])
    return sent_to_all(pair, "zq")


def over_plane(block):
    return sent_to_all(block, ("x", "y")).reshape((4,) * 3 + block.shape[1:])


def lat_shift(value, by):
    perm = [(i, (i + by) % 32) for i in range(32)]
    return lax.ppermute(value, ("za", "zq", "x"), perm)


def lon_shift(value, by):
    perm = [(i, (i + by) % 8) for i in range(8)]
    return lax.ppermute(value, ("y", "zh"), perm)


def window_kernel(tokens, left_weight, right_weight, bias, out):
    normed = tokens[0]
    left = jnp.dot(normed, left_weight[...], preferred_element_type=jnp.float32)
    left = left.astype(jnp.bfloat16)
    right = jnp.dot(normed, right_weight[:, :128], preferred_element_type=jnp.float32)
    right = right.astype(jnp.bfloat16)
    lower = lax.broadcasted_iota(jnp.int32, (1, 2 * HEAD), 1) < HEAD
    values = (left[:, 512:640], right)
    for pair in range(2):
        query = left[:, 128 * pair : 128 * (pair + 1)]
        keys = left[:, 256 + 128 * pair : 256 + 128 * (pair + 1)]
        mixed = []
        for keep in (lower, ~lower):
            kept = query * jnp.where(keep, HEAD**-0.5, 0.0).astype(jnp.bfloat16)
            scores = lax.dot_general(
                kept, keys, (((1,), (1,)), ((), ())), preferred_element_type=jnp.float32
            )
            scores = scores + bias[0]
            weights = jnp.exp(scores - jnp.max(scores, axis=-1, keepdims=True))
            total = jnp.sum(weights, axis=-1, keepdims=True)
            mixed.append(
                jnp.dot(
                    weights.astype(jnp.bfloat16), values[pair], preferred_element_type=jnp.float32
                )
                / total
            )
        out[0, :, 128 * pair : 128 * (pair + 1)] = jnp.where(lower, *mixed).astype(jnp.bfloat16)


def fine_windows(tokens, left_weight, right_weight, bias):
    windows, size, features = tokens.shape
    flops = 2 * windows * size * (features * 768 + 4 * size * 128 * 2)
    return pl.pallas_call(
        window_kernel,
        grid=(windows,),
        in_specs=[
            pl.BlockSpec((1, size, features), lambda i: (i, 0, 0)),
            pl.BlockSpec(left_weight.shape, lambda i: (0, 0)),
            pl.BlockSpec(right_weight.shape, lambda i: (0, 0)),
            pl.BlockSpec((1, size, size), lambda i: (i // 3, 0, 0)),
        ],
        out_specs=pl.BlockSpec((1, size, 256), lambda i: (i, 0, 0)),
        out_shape=jax.ShapeDtypeStruct((windows, size, 256), jnp.bfloat16),
        compiler_params=pltpu.CompilerParams(vmem_limit_bytes=16 * 2**20),
        cost_estimate=pl.CostEstimate(
            flops=flops, bytes_accessed=4 * 2**20, transcendentals=windows * 4 * size * size
        ),
    )(tokens, left_weight, right_weight, bias)


def body(
    fine_tokens,
    attn_gain,
    fine_qkv,
    fine_proj,
    merge_gain,
    merge_weight,
    coarse_gain,
    coarse_qkv,
    coarse_proj,
    split_weight,
    split_gain,
):
    levels, row_count, col_count, features = fine_tokens.shape
    lat_total = row_count * 32
    row_first = lax.axis_index(("za", "zq", "x")) * row_count
    rim_rows = WIN_LAT // 2
    rim_cols = WIN_LON // 2

    core = lax.axis_index("core")
    packed_width = 3 * fine_qkv.shape[2]
    first_shard = jnp.concatenate([fine_qkv.reshape(16, packed_width), fine_proj.T], axis=1)
    merge_part = quartered(merge_weight, 4, 1)
    late_shard = jnp.concatenate([split_weight.reshape(32, -1), coarse_proj.T], axis=1)
    late_shard = jnp.pad(late_shard, ((0, 56), (0, 0)))
    early = jnp.concatenate(
        [
            quartered(first_shard, 2, 2),
            merge_part[:8],
            merge_part[8:],
            quartered(coarse_qkv.reshape(32, -1), 4, 1),
        ],
        axis=1,
    )
    early, late_shard = lax.optimization_barrier((early, late_shard))
    depth = over_depth(early)
    late = lax.all_gather(late_shard, "x", axis=0, tiled=False)
    late = late[:, :32].reshape(128, 1536)

    own_half = lax.dynamic_slice_in_dim(
        fine_tokens, core * (features // 2), features // 2, 3
    )
    east = lon_shift(own_half[:, :, :rim_cols], -1)
    west = lon_shift(own_half[:, :, col_count - rim_cols :], 1)
    strip = jnp.concatenate([west, own_half, east], axis=2)
    below = lat_shift(strip[:, :rim_rows], -1)
    above = lat_shift(strip[:, row_count - rim_rows :], 1)
    rims = [above, below, west, east]
    flat_rims = lax.all_gather(
        jnp.concatenate([rim.reshape(-1, features // 2) for rim in rims], axis=0),
        "core",
        axis=1,
        tiled=True,
    )
    whole, place = [], 0
    for rim in rims:
        rows = rim.size // (features // 2)
        whole.append(flat_rims[place : place + rows].reshape(rim.shape[:3] + (features,)))
        place += rows
    above, below, west, east = whole
    extended = jnp.concatenate(
        [above, jnp.concatenate([west, fine_tokens, east], axis=2), below], axis=1
    )
    wide_rows, wide_cols = extended.shape[1:3]
    window_rows, window_cols = wide_rows // WIN_LAT, wide_cols // WIN_LON
    size = levels * WIN_LAT * WIN_LON
    normed = layer_norm(extended.astype(jnp.float32), attn_gain).astype(jnp.bfloat16)
    normed = normed.reshape(levels, window_rows, WIN_LAT, window_cols, WIN_LON, features)
    normed = normed.transpose(1, 3, 0, 2, 4, 5).reshape(-1, size, features)
    global_rows = row_first - rim_rows + jnp.arange(wide_rows, dtype=jnp.int32)
    global_rows = (global_rows + lat_total) % lat_total
    labels = seam_labels(global_rows, lat_total, rim_rows).reshape(window_rows, 1, WIN_LAT, 1)
    labels = jnp.broadcast_to(labels, (window_rows, levels, WIN_LAT, WIN_LON))
    labels = labels.reshape(window_rows, size)
    bias = jnp.where(labels[:, :, None] == labels[:, None, :], 0.0, -1e30).astype(jnp.float32)

    depth, normed, bias, late = lax.optimization_barrier((depth, normed, bias, late))
    first_all = over_plane(depth[..., :640])
    late = lax.all_gather(late, ("za", "zq"), axis=0, tiled=True)
    depth, first_all = lax.optimization_barrier((depth, first_all))
    merge_all = over_plane(depth[..., 640:1664])
    first_all = first_all.reshape(4, 2, 2, 4, 2, 8, 640)
    left_weight, right_weight = (
        first_all[:, :, part].transpose(3, 2, 0, 1, 4, 5).reshape(512, 640) for part in range(2)
    )
    window_out = fine_windows(normed, left_weight, right_weight, bias)
    depth, window_out, merge_all = lax.optimization_barrier((depth, window_out, merge_all))
    qkv_all = over_plane(depth[..., 1664:])
    merge_all = jnp.stack([merge_all[..., :512], merge_all[..., 512:]], axis=4)
    merge_all = merge_all.transpose(3, 2, 0, 1, 4, 5, 6).reshape(2048, 512)
    qkv_all = qkv_all.transpose(3, 2, 0, 1, 4, 5).reshape(1024, 1536)
    window_out = window_out.reshape(window_rows, window_cols, levels, WIN_LAT, WIN_LON, 256)
    window_out = window_out.transpose(2, 0, 3, 1, 4, 5).reshape(levels, wide_rows, wide_cols, 256)
    window_out = window_out[
        :, rim_rows : rim_rows + row_count, rim_cols : rim_cols + col_count
    ]
    all_heads = lax.all_gather(window_out, "core", axis=3, tiled=True).reshape(-1, features)
    attended = project_with_transposed(all_heads, right_weight[:, 128:])
    flat_tokens = fine_tokens.reshape(-1, features)
    residual = (flat_tokens.astype(jnp.float32) + attended).astype(jnp.bfloat16)
    half_rows = row_count // 2
    half_cols = col_count // 2
    quartets = (
        residual.reshape(levels, half_rows, 2, half_cols, 2, features)
        .transpose(0, 1, 3, 2, 4, 5)
        .reshape(-1, 4 * features)
    )
    merged_in = layer_norm(quartets.astype(jnp.float32), merge_gain).astype(jnp.bfloat16)
    coarse_rows = merged_in.shape[0]
    coarse_half = project_with(merged_in, merge_all).astype(jnp.bfloat16)
    coarse_full = lax.all_gather(coarse_half, "core", axis=1, tiled=True)
    coarse_normed = layer_norm(coarse_full.astype(jnp.float32), coarse_gain).astype(jnp.bfloat16)
    coarse_packed = project_with(coarse_normed, qkv_all).astype(jnp.bfloat16)
    heads_here = coarse_qkv.shape[2] // HEAD
    coarse_mixed = window_mix(
        coarse_packed.reshape(levels, half_rows, half_cols, -1), heads_here, None
    ).reshape(coarse_rows, -1)
    partial_value = project_with_transposed(coarse_mixed, late[:, 1024:]).astype(jnp.bfloat16)
    both = lax.all_gather(partial_value, "core", axis=0, tiled=False).astype(jnp.float32)
    coarse_out = (coarse_full.astype(jnp.float32) + (both[0] + both[1])).astype(jnp.bfloat16)
    feature_half = split_weight.shape[2]
    expanded = project_with(coarse_out, late[:, :1024])
    expanded = expanded.reshape(coarse_rows, 4, feature_half)
    first_sum, second_sum = lax.psum(
        (jnp.sum(expanded, axis=-1), jnp.sum(expanded * expanded, axis=-1)), "core"
    )
    average = first_sum / features
    spread = second_sum / features - average * average
    feature_start = core * feature_half
    gain_part = lax.dynamic_slice_in_dim(split_gain, feature_start, feature_half, 0)
    normed_split = (
        (expanded - average[..., None]) * lax.rsqrt(spread[..., None] + EPSILON) * gain_part
    )
    restored = (
        normed_split.reshape(levels, half_rows, half_cols, 2, 2, feature_half)
        .transpose(0, 1, 3, 2, 4, 5)
        .reshape(levels, row_count, col_count, feature_half)
    )
    skip_part = lax.dynamic_slice_in_dim(
        residual.reshape(levels, row_count, col_count, features), feature_start, feature_half, 3
    )
    return (skip_part.astype(jnp.float32) + restored).astype(jnp.bfloat16)


def solution(mesh):
    finer = Mesh(
        mesh.devices.reshape(2, 4, 4, 4, 2, 2), ("za", "zq", "x", "y", "zh", "core")
    )
    lat, lon, tp = ("za", "zq", "x"), ("y", "zh"), "core"
    in_specs = (
        P(None, lat, lon, None),
        P(),
        P(lat, None, tp),
        P(None, lat),
        P(),
        P(lat, tp),
        P(),
        P(lat, None, tp),
        P(tp, lat),
        P(lat, None, tp),
        P(),
    )
    out_specs = P(None, lat, lon, tp)
    return jax.shard_map(body, mesh=finer, in_specs=in_specs, out_specs=out_specs, check_vma=False)
```

```python
import jax
import jax.numpy as jnp
import numpy as np
from jax import lax
from jax.experimental import pallas as pl
from jax.experimental.pallas import tpu as pltpu
from jax.sharding import Mesh, PartitionSpec as P

HEAD = 64
WIN_LAT = 6
WIN_LON = 12


EPSILON = 1e-05

LEVELS, ROWS, COLS = 2, 12, 24
RIM_ROWS, RIM_COLS = WIN_LAT // 2, WIN_LON // 2
OWN = LEVELS * ROWS * COLS
SIDE = LEVELS * ROWS * RIM_COLS
ENDS = LEVELS * RIM_ROWS * (COLS + 2 * RIM_COLS)
RIMS = 2 * SIDE + 2 * ENDS
WINDOW = LEVELS * WIN_LAT * WIN_LON
COARSE = OWN // 4


def wide_places():
    wide = np.zeros((LEVELS, ROWS + 2 * RIM_ROWS, COLS + 2 * RIM_COLS), np.int32)
    rows, cols = slice(RIM_ROWS, RIM_ROWS + ROWS), slice(RIM_COLS, RIM_COLS + COLS)
    start = 0
    for part in (
        wide[:, rows, cols],
        wide[:, rows, :RIM_COLS],
        wide[:, rows, RIM_COLS + COLS :],
        wide[:, :RIM_ROWS],
        wide[:, RIM_ROWS + ROWS :],
    ):
        part[...] = start + np.arange(part.size).reshape(part.shape)
        start += part.size
    return wide


WIDE = wide_places()
OWN_ROWS = slice(RIM_ROWS, RIM_ROWS + ROWS)
FIRST_COLS = WIDE[:, OWN_ROWS, RIM_COLS : 2 * RIM_COLS].reshape(-1, 1)
LAST_COLS = WIDE[:, OWN_ROWS, COLS : COLS + RIM_COLS].reshape(-1, 1)
FIRST_ROWS = WIDE[:, RIM_ROWS : 2 * RIM_ROWS].reshape(-1, 1)
LAST_ROWS = WIDE[:, ROWS : ROWS + RIM_ROWS].reshape(-1, 1)
WINDOWS = (
    WIDE.reshape(LEVELS, 3, WIN_LAT, 3, WIN_LON).transpose(1, 3, 0, 2, 4).reshape(9, WINDOW)
)
QUARTETS = (
    np.arange(OWN, dtype=np.int32)
    .reshape(LEVELS, ROWS // 2, 2, COLS // 2, 2)
    .transpose(2, 4, 0, 1, 3)
    .reshape(4, COARSE)
)


def layer_norm(values, gain_row):
    average = jnp.mean(values, axis=-1, keepdims=True)
    centred = values - average
    spread = jnp.mean(centred * centred, axis=-1, keepdims=True)
    return centred * lax.rsqrt(spread + EPSILON) * gain_row


def seam_labels(global_rows, lat_total, rim_rows):
    return jnp.where(
        global_rows >= lat_total - rim_rows, 1, jnp.where(global_rows < rim_rows, 2, 0)
    ).astype(jnp.int32)


def project_with(left_side, fragment):
    return jnp.dot(left_side, fragment, preferred_element_type=jnp.float32)


def project_with_transposed(left_side, fragment):
    return lax.dot_general(
        left_side, fragment, (((1,), (1,)), ((), ())), preferred_element_type=jnp.float32
    )


def picked(column, count):
    places = lax.broadcasted_iota(jnp.int32, (column.shape[0], count), 1)
    return (places == column).astype(jnp.bfloat16)


def spread_out(row, count):
    places = lax.broadcasted_iota(jnp.int32, (count, row.shape[1]), 0)
    return (places == row).astype(jnp.bfloat16)


def pair_mix(query, keys, values, lower, bias):
    mixed = []
    for keep in (lower, ~lower):
        kept = query * jnp.where(keep, HEAD**-0.5, 0.0).astype(jnp.bfloat16)
        scores = project_with_transposed(kept, keys)
        if bias is not None:
            scores = scores + bias
        weights = jnp.exp(scores - jnp.max(scores, axis=-1, keepdims=True))
        total = jnp.sum(weights, axis=-1, keepdims=True)
        mixed.append(project_with(weights.astype(jnp.bfloat16), values) / total)
    return jnp.where(lower, *mixed)


def call(kernel, out_shape, operands, scalars=0, limit=24, flops=10**8, **options):
    whole = pl.BlockSpec(memory_space=pltpu.VMEM)
    options.setdefault(
        "in_specs",
        [pl.BlockSpec(memory_space=pltpu.SMEM)] * scalars + [whole] * (len(operands) - scalars),
    )
    options.setdefault("out_specs", jax.tree.map(lambda _: whole, out_shape))
    return pl.pallas_call(
        kernel,
        out_shape=out_shape,
        compiler_params=pltpu.CompilerParams(vmem_limit_bytes=limit * 2**20),
        cost_estimate=pl.CostEstimate(flops=flops, bytes_accessed=2**20, transcendentals=0),
        **options,
    )(*operands)


def shape(*sizes, dtype=jnp.bfloat16):
    return jax.ShapeDtypeStruct(sizes, dtype)


def pack_kernel(place, fine_qkv, fine_proj, merge, coarse_qkv, coarse_proj, split, early, late):
    y = place[0]
    wide = jnp.concatenate(
        [fine_qkv[:, part, :].astype(jnp.float32) for part in range(3)]
        + [fine_proj[...].astype(jnp.float32)],
        axis=1,
    )
    half = jnp.where(y >= 2, wide[8:], wide[:8])
    odd = (y == 1) | (y == 3)
    early[:, :640] = jnp.where(odd, half[:, 640:], half[:, :640]).astype(jnp.bfloat16)
    rows = merge[pl.ds(pl.multiple_of(y * 16, 16), 16), :].astype(jnp.float32)
    early[:, 640:1152] = rows[:8].astype(jnp.bfloat16)
    early[:, 1152:1664] = rows[8:].astype(jnp.bfloat16)
    for part in range(3):
        cols = coarse_qkv[:, part, pl.ds(pl.multiple_of(y * 128, 128), 128)].astype(jnp.float32)
        for block in range(4):
            start = 1664 + 384 * block + 128 * part
            early[:, start : start + 128] = cols[8 * block : 8 * block + 8].astype(jnp.bfloat16)
    late[...] = jnp.zeros_like(late)
    for part in range(4):
        late[:32, 256 * part : 256 * (part + 1)] = split[:, part, :]
    late[:32, 1024:] = coarse_proj[...]


def norm_kernel(core, tokens, gain, first_place, last_place, normed, first, last):
    values = layer_norm(tokens[...].astype(jnp.float32), gain[...]).astype(jnp.bfloat16)
    normed[...] = values
    half = jnp.where(core[0] == 0, values[:, :256], values[:, 256:])
    first[...] = project_with(picked(first_place[...], OWN), half).astype(jnp.bfloat16)
    last[...] = project_with(picked(last_place[...], OWN), half).astype(jnp.bfloat16)


def ends_kernel(core, normed, west, east, first_place, last_place, first, last):
    half = jnp.where(core[0] == 0, normed[:, :256], normed[:, 256:])
    for place, out in ((first_place, first), (last_place, last)):
        pick = picked(place[...], OWN + 2 * SIDE)
        rows = project_with(pick[:, :OWN], half)
        rows += project_with(pick[:, OWN : OWN + SIDE], west[...])
        rows += project_with(pick[:, OWN + SIDE :], east[...])
        out[...] = rows.astype(jnp.bfloat16)


def fine_kernel(normed, rims, left_weight, right_weight, bias, column, row, out, total):
    window = pl.program_id(0)
    pick = picked(column[0], OWN + RIMS)
    tokens = project_with(pick[:, :OWN], normed[...]) + project_with(pick[:, OWN:], rims[...])
    tokens = tokens.astype(jnp.bfloat16)
    left = project_with(tokens, left_weight[...]).astype(jnp.bfloat16)
    right = project_with(tokens, right_weight[:, :128]).astype(jnp.bfloat16)
    lower = lax.broadcasted_iota(jnp.int32, (1, 2 * HEAD), 1) < HEAD
    values = (left[:, 512:640], right)
    mixed = [
        pair_mix(
            left[:, 128 * pair : 128 * (pair + 1)],
            left[:, 256 + 128 * pair : 256 + 128 * (pair + 1)],
            values[pair],
            lower,
            bias[0],
        ).astype(jnp.bfloat16)
        for pair in range(2)
    ]

    @pl.when(window == 0)
    def _():
        total[...] = jnp.zeros_like(total)

    total[...] += project_with(spread_out(row[0], OWN), jnp.concatenate(mixed, axis=1))

    @pl.when(window == 8)
    def _():
        out[...] = total[...].astype(jnp.bfloat16)


def merge_kernel(heads, weight, tokens, gain, places, residual, merged):
    attended = project_with_transposed(heads[...], weight[:, 128:])
    values = (tokens[...].astype(jnp.float32) + attended).astype(jnp.bfloat16)
    residual[...] = values
    quartet = jnp.concatenate(
        [project_with(picked(places[part], OWN), values) for part in range(4)], axis=1
    )
    merged[...] = layer_norm(quartet, gain[...]).astype(jnp.bfloat16)


def coarse_kernel(order, coarse, gain, row_order, first, second, third, fourth, out):
    normed = layer_norm(coarse[...].astype(jnp.float32), gain[...]).astype(jnp.bfloat16)
    normed = project_with(normed, row_order[...]).astype(jnp.bfloat16)
    lower = lax.broadcasted_iota(jnp.int32, (1, 2 * HEAD), 1) < HEAD
    for place, piece in enumerate((first, second, third, fourth)):
        packed = jnp.zeros((normed.shape[0], 384), jnp.float32)
        for part in range(4):
            packed += project_with(
                normed[:, 256 * part : 256 * (part + 1)], piece[:, 384 * part : 384 * (part + 1)]
            )
        packed = packed.astype(jnp.bfloat16)
        mixed = pair_mix(packed[:, :128], packed[:, 128:256], packed[:, 256:], lower, None)
        out[order[place]] = mixed.astype(jnp.bfloat16)


def final_kernel(core, expanded, first_sum, second_sum, gain, residual, places, out):
    half = jnp.where(core[0] == 0, residual[:, :256], residual[:, 256:]).astype(jnp.float32)
    own_gain = jnp.where(core[0] == 0, gain[:, :256], gain[:, 256:])
    total = half
    for part in range(4):
        average = first_sum[:, part : part + 1] / 512
        spread = second_sum[:, part : part + 1] / 512 - average * average
        values = expanded[:, 256 * part : 256 * (part + 1)] - average
        values = values * lax.rsqrt(spread + EPSILON) * own_gain
        high = values.astype(jnp.bfloat16)
        low = (values - high.astype(jnp.float32)).astype(jnp.bfloat16)
        back = spread_out(places[part], OWN)
        total = total + (project_with(back, high) + project_with(back, low))
    out[...] = total.astype(jnp.bfloat16)


def sent_to_all(block, axes):
    peers = lax.axis_size(axes)
    copies = jnp.broadcast_to(block[None], (peers,) + block.shape)
    return lax.all_to_all(copies, axes, split_axis=0, concat_axis=0, tiled=True)


def over_depth(block):
    other = lax.ppermute(block, "za", [(0, 1), (1, 0)])
    upper = lax.axis_index("za") == 1
    pair = jnp.stack([jnp.where(upper, other, block), jnp.where(upper, block, other)])
    return sent_to_all(pair, "zq")


def from_others(block, axis):
    return [block] + [
        lax.ppermute(block, axis, [((i + by) % 4, i) for i in range(4)]) for by in (1, 2, 3)
    ]


def lat_shift(value, by):
    perm = [(i, (i + by) % 32) for i in range(32)]
    return lax.ppermute(value, ("za", "zq", "x"), perm)


def lon_shift(value, by):
    perm = [(i, (i + by) % 8) for i in range(8)]
    return lax.ppermute(value, ("y", "zh"), perm)


def body(
    fine_tokens,
    attn_gain,
    fine_qkv,
    fine_proj,
    merge_gain,
    merge_weight,
    coarse_gain,
    coarse_qkv,
    coarse_proj,
    split_weight,
    split_gain,
):
    lat_total = ROWS * 32
    row_first = lax.axis_index(("za", "zq", "x")) * ROWS
    core = lax.axis_index("core").astype(jnp.int32)[None]
    x_place, y_place = lax.axis_index("x"), lax.axis_index("y")
    flat_tokens = fine_tokens.reshape(OWN, 512)

    early, late_shard = call(
        pack_kernel,
        (shape(8, 3200), shape(88, 1536)),
        (
            y_place.astype(jnp.int32)[None],
            fine_qkv,
            fine_proj.T,
            merge_weight,
            coarse_qkv,
            coarse_proj.T,
            split_weight,
        ),
        scalars=1,
    )
    late = lax.all_gather(late_shard, "x", axis=0, tiled=False)
    late = late[:, :32].reshape(128, 1536)

    normed, first_cols, last_cols = call(
        norm_kernel,
        (shape(OWN, 512), shape(SIDE, 256), shape(SIDE, 256)),
        (core, flat_tokens, attn_gain[None], FIRST_COLS, LAST_COLS),
        scalars=1,
    )
    east = lon_shift(first_cols, -1)
    west = lon_shift(last_cols, 1)
    early, east, west = lax.optimization_barrier((early, east, west))
    first_rows, last_rows = call(
        ends_kernel,
        (shape(ENDS, 256), shape(ENDS, 256)),
        (core, normed, west, east, FIRST_ROWS, LAST_ROWS),
        scalars=1,
    )
    below = lat_shift(first_rows, -1)
    above = lat_shift(last_rows, 1)
    depth = over_depth(early)
    depth, above, below, late = lax.optimization_barrier((depth, above, below, late))
    late = lax.all_gather(late, ("za", "zq"), axis=0, tiled=True)

    rims = jnp.concatenate([west, east, above, below], axis=0)
    rims = lax.all_gather(rims, "core", axis=1, tiled=True)
    global_rows = row_first - RIM_ROWS + jnp.arange(ROWS + 2 * RIM_ROWS, dtype=jnp.int32)
    labels = seam_labels((global_rows + lat_total) % lat_total, lat_total, RIM_ROWS)
    labels = labels.reshape(3, 1, WIN_LAT, 1)
    labels = jnp.broadcast_to(labels, (3, LEVELS, WIN_LAT, WIN_LON)).reshape(3, WINDOW)
    bias = jnp.where(labels[:, :, None] == labels[:, None, :], 0.0, -1e30).astype(jnp.float32)

    merge_side = sent_to_all(depth[..., :1664], "y")
    qkv_quad = jnp.stack(from_others(depth[..., 1664:], "x")).reshape(256, 1536)
    merge_side, qkv_quad = lax.optimization_barrier((merge_side, qkv_quad))
    qkv_pieces = from_others(qkv_quad, "y")
    first_all = sent_to_all(merge_side[..., :640], "x")
    merge_side, first_all = lax.optimization_barrier((merge_side, first_all))
    merge_all = sent_to_all(merge_side[..., 640:], "x")
    first_all = first_all.reshape(4, 2, 2, 4, 2, 8, 640)
    left_weight, right_weight = (
        first_all[:, :, part].transpose(3, 2, 0, 1, 4, 5).reshape(512, 640) for part in range(2)
    )

    constant = lambda i: (0, 0)
    window_out = call(
        fine_kernel,
        shape(OWN, 256),
        (normed, rims, left_weight, right_weight, bias, WINDOWS[:, :, None], WINDOWS[:, None, :]),
        grid=(9,),
        in_specs=[
            pl.BlockSpec((OWN, 512), constant),
            pl.BlockSpec((RIMS, 512), constant),
            pl.BlockSpec((512, 640), constant),
            pl.BlockSpec((512, 640), constant),
            pl.BlockSpec((1, WINDOW, WINDOW), lambda i: (i // 3, 0, 0)),
            pl.BlockSpec((1, WINDOW, 1), lambda i: (i, 0, 0)),
            pl.BlockSpec((1, 1, WINDOW), lambda i: (i, 0, 0)),
        ],
        out_specs=pl.BlockSpec((OWN, 256), constant),
        scratch_shapes=[pltpu.VMEM((OWN, 256), jnp.float32)],
    )
    all_heads = lax.all_gather(window_out, "core", axis=1, tiled=True)
    residual, merged_in = call(
        merge_kernel,
        (shape(OWN, 512), shape(COARSE, 2048)),
        (all_heads, right_weight, flat_tokens, merge_gain[None], QUARTETS[:, :, None]),
    )
    merge_all, qkv_pieces = lax.optimization_barrier((merge_all, qkv_pieces))
    merge_all = merge_all.reshape(4, 4, 4, 2, 8, 1024)
    merge_all = jnp.stack([merge_all[..., :512], merge_all[..., 512:]], axis=4)
    merge_all = merge_all.transpose(3, 2, 0, 1, 4, 5, 6).reshape(2048, 512)
    coarse_half = project_with(merged_in, merge_all).astype(jnp.bfloat16)
    coarse_full = lax.all_gather(coarse_half, "core", axis=1, tiled=True)

    place = jnp.arange(1024, dtype=jnp.int32)
    feature = place // 8 % 2 * 512 + place // 16 % 4 * 128 + (place // 64 + x_place) % 4 * 32
    feature = feature + place // 256 * 8 + place % 8
    row_order = (place[:, None] == feature[None, :]).astype(jnp.bfloat16)
    qkv_pieces, late = lax.optimization_barrier((qkv_pieces, late))
    order = (y_place + jnp.arange(4, dtype=jnp.int32)) % 4
    coarse_mixed = call(
        coarse_kernel,
        shape(4, COARSE, 128),
        (order, coarse_full, coarse_gain[None], row_order, *qkv_pieces),
        scalars=1,
    )
    coarse_mixed = coarse_mixed.transpose(1, 0, 2).reshape(COARSE, 512)
    partial_value = project_with_transposed(coarse_mixed, late[:, 1024:]).astype(jnp.bfloat16)
    both = lax.all_gather(partial_value, "core", axis=0, tiled=False).astype(jnp.float32)
    coarse_out = (coarse_full.astype(jnp.float32) + (both[0] + both[1])).astype(jnp.bfloat16)
    expanded = project_with(coarse_out, late[:, :1024])
    parts = expanded.reshape(COARSE, 4, 256)
    first_sum, second_sum = lax.psum(
        (jnp.sum(parts, axis=-1), jnp.sum(parts * parts, axis=-1)), "core"
    )
    restored = call(
        final_kernel,
        shape(OWN, 256),
        (
            core,
            expanded,
            first_sum,
            second_sum,
            split_gain[None],
            residual,
            QUARTETS[:, None, :],
        ),
        scalars=1,
    )
    return restored.reshape(LEVELS, ROWS, COLS, 256)


def solution(mesh):
    finer = Mesh(
        mesh.devices.reshape(2, 4, 4, 4, 2, 2), ("za", "zq", "x", "y", "zh", "core")
    )
    lat, lon, tp = ("za", "zq", "x"), ("y", "zh"), "core"
    in_specs = (
        P(None, lat, lon, None),
        P(),
        P(lat, None, tp),
        P(None, lat),
        P(),
        P(lat, tp),
        P(),
        P(lat, None, tp),
        P(tp, lat),
        P(lat, None, tp),
        P(),
    )
    out_specs = P(None, lat, lon, tp)
    return jax.shard_map(body, mesh=finer, in_specs=in_specs, out_specs=out_specs, check_vma=False)
```

```python
import jax
import jax.numpy as jnp
import numpy as np
from jax import lax
from jax.experimental import pallas as pl
from jax.experimental.pallas import tpu as pltpu
from jax.sharding import Mesh, PartitionSpec as P

HEAD = 64
WIN_LAT = 6
WIN_LON = 12


EPSILON = 1e-05

LEVELS, ROWS, COLS = 2, 12, 24
RIM_ROWS, RIM_COLS = WIN_LAT // 2, WIN_LON // 2
OWN = LEVELS * ROWS * COLS
SIDE = LEVELS * ROWS * RIM_COLS
ENDS = LEVELS * RIM_ROWS * (COLS + 2 * RIM_COLS)
RIMS = 2 * SIDE + 2 * ENDS
WINDOW = LEVELS * WIN_LAT * WIN_LON
COARSE = OWN // 4


def wide_places():
    wide = np.zeros((LEVELS, ROWS + 2 * RIM_ROWS, COLS + 2 * RIM_COLS), np.int32)
    rows, cols = slice(RIM_ROWS, RIM_ROWS + ROWS), slice(RIM_COLS, RIM_COLS + COLS)
    start = 0
    for part in (
        wide[:, rows, cols],
        wide[:, rows, :RIM_COLS],
        wide[:, rows, RIM_COLS + COLS :],
        wide[:, :RIM_ROWS],
        wide[:, RIM_ROWS + ROWS :],
    ):
        part[...] = start + np.arange(part.size).reshape(part.shape)
        start += part.size
    return wide


WIDE = wide_places()
OWN_ROWS = slice(RIM_ROWS, RIM_ROWS + ROWS)
FIRST_COLS = WIDE[:, OWN_ROWS, RIM_COLS : 2 * RIM_COLS].reshape(-1, 1)
LAST_COLS = WIDE[:, OWN_ROWS, COLS : COLS + RIM_COLS].reshape(-1, 1)
FIRST_ROWS = WIDE[:, RIM_ROWS : 2 * RIM_ROWS].reshape(-1, 1)
LAST_ROWS = WIDE[:, ROWS : ROWS + RIM_ROWS].reshape(-1, 1)
WINDOWS = (
    WIDE.reshape(LEVELS, 3, WIN_LAT, 3, WIN_LON).transpose(1, 3, 0, 2, 4).reshape(9, WINDOW)
)
QUARTETS = (
    np.arange(OWN, dtype=np.int32)
    .reshape(LEVELS, ROWS // 2, 2, COLS // 2, 2)
    .transpose(2, 4, 0, 1, 3)
    .reshape(4, COARSE)
)


def layer_norm(values, gain_row):
    average = jnp.mean(values, axis=-1, keepdims=True)
    centred = values - average
    spread = jnp.mean(centred * centred, axis=-1, keepdims=True)
    return centred * lax.rsqrt(spread + EPSILON) * gain_row


def seam_labels(global_rows, lat_total, rim_rows):
    return jnp.where(
        global_rows >= lat_total - rim_rows, 1, jnp.where(global_rows < rim_rows, 2, 0)
    ).astype(jnp.int32)


def project_with(left_side, fragment):
    return jnp.dot(left_side, fragment, preferred_element_type=jnp.float32)


def project_with_transposed(left_side, fragment):
    return lax.dot_general(
        left_side, fragment, (((1,), (1,)), ((), ())), preferred_element_type=jnp.float32
    )


def picked(column, count):
    places = lax.broadcasted_iota(jnp.int32, (column.shape[0], count), 1)
    return (places == column).astype(jnp.bfloat16)


def spread_out(row, count):
    places = lax.broadcasted_iota(jnp.int32, (count, row.shape[1]), 0)
    return (places == row).astype(jnp.bfloat16)


def pair_mix(query, keys, values, lower, bias):
    mixed = []
    for keep in (lower, ~lower):
        kept = query * jnp.where(keep, HEAD**-0.5, 0.0).astype(jnp.bfloat16)
        scores = project_with_transposed(kept, keys)
        if bias is not None:
            scores = scores + bias
        weights = jnp.exp(scores - jnp.max(scores, axis=-1, keepdims=True))
        total = jnp.sum(weights, axis=-1, keepdims=True)
        mixed.append(project_with(weights.astype(jnp.bfloat16), values) / total)
    return jnp.where(lower, *mixed)


def call(kernel, out_shape, operands, scalars=0, limit=24, flops=10**8, **options):
    whole = pl.BlockSpec(memory_space=pltpu.VMEM)
    options.setdefault(
        "in_specs",
        [pl.BlockSpec(memory_space=pltpu.SMEM)] * scalars + [whole] * (len(operands) - scalars),
    )
    options.setdefault("out_specs", jax.tree.map(lambda _: whole, out_shape))
    return pl.pallas_call(
        kernel,
        out_shape=out_shape,
        compiler_params=pltpu.CompilerParams(vmem_limit_bytes=limit * 2**20),
        cost_estimate=pl.CostEstimate(flops=flops, bytes_accessed=2**20, transcendentals=0),
        **options,
    )(*operands)


def shape(*sizes, dtype=jnp.bfloat16):
    return jax.ShapeDtypeStruct(sizes, dtype)


def pack_kernel(place, fine_qkv, fine_proj, merge, coarse_qkv, coarse_proj, split, early, late):
    y = place[0]
    wide = jnp.concatenate(
        [fine_qkv[:, part, :].astype(jnp.float32) for part in range(3)]
        + [fine_proj[...].astype(jnp.float32)],
        axis=1,
    )
    half = jnp.where(y >= 2, wide[8:], wide[:8])
    odd = (y == 1) | (y == 3)
    early[:, :640] = jnp.where(odd, half[:, 640:], half[:, :640]).astype(jnp.bfloat16)
    rows = merge[pl.ds(pl.multiple_of(y * 16, 16), 16), :].astype(jnp.float32)
    early[:, 640:1152] = rows[:8].astype(jnp.bfloat16)
    early[:, 1152:1664] = rows[8:].astype(jnp.bfloat16)
    for part in range(3):
        cols = coarse_qkv[:, part, pl.ds(pl.multiple_of(y * 128, 128), 128)].astype(jnp.float32)
        for block in range(4):
            start = 1664 + 384 * block + 128 * part
            early[:, start : start + 128] = cols[8 * block : 8 * block + 8].astype(jnp.bfloat16)
    late[...] = jnp.zeros_like(late)
    for part in range(4):
        late[:32, 256 * part : 256 * (part + 1)] = split[:, part, :]
    late[:32, 1024:] = coarse_proj[...]


def norm_kernel(core, tokens, gain, first_place, last_place, normed, first, last):
    values = layer_norm(tokens[...].astype(jnp.float32), gain[...]).astype(jnp.bfloat16)
    normed[...] = values
    half = jnp.where(core[0] == 0, values[:, :256], values[:, 256:])
    first[...] = project_with(picked(first_place[...], OWN), half).astype(jnp.bfloat16)
    last[...] = project_with(picked(last_place[...], OWN), half).astype(jnp.bfloat16)


def ends_kernel(core, normed, west, east, first_place, last_place, first, last):
    half = jnp.where(core[0] == 0, normed[:, :256], normed[:, 256:])
    for place, out in ((first_place, first), (last_place, last)):
        pick = picked(place[...], OWN + 2 * SIDE)
        rows = project_with(pick[:, :OWN], half)
        rows += project_with(pick[:, OWN : OWN + SIDE], west[...])
        rows += project_with(pick[:, OWN + SIDE :], east[...])
        out[...] = rows.astype(jnp.bfloat16)


def window_kernel(normed, rims, column, out):
    pick = picked(column[0], OWN + RIMS)
    rows = project_with(pick[:, :OWN], normed[...]) + project_with(pick[:, OWN:], rims[...])
    out[0] = rows.astype(jnp.bfloat16)


def fine_kernel(windows, left_weight, right_weight, bias, row, out, total):
    window = pl.program_id(0)
    tokens = windows[0]
    left = project_with(tokens, left_weight[...]).astype(jnp.bfloat16)
    right = project_with(tokens, right_weight[:, :128]).astype(jnp.bfloat16)
    lower = lax.broadcasted_iota(jnp.int32, (1, 2 * HEAD), 1) < HEAD
    values = (left[:, 512:640], right)
    mixed = [
        pair_mix(
            left[:, 128 * pair : 128 * (pair + 1)],
            left[:, 256 + 128 * pair : 256 + 128 * (pair + 1)],
            values[pair],
            lower,
            bias[0],
        ).astype(jnp.bfloat16)
        for pair in range(2)
    ]

    @pl.when(window == 0)
    def _():
        total[...] = jnp.zeros_like(total)

    total[...] += project_with(spread_out(row[0], OWN), jnp.concatenate(mixed, axis=1))

    @pl.when(window == 8)
    def _():
        out[...] = total[...].astype(jnp.bfloat16)


def merge_kernel(heads, weight, tokens, gain, places, residual, merged):
    attended = project_with_transposed(heads[...], weight[:, 128:])
    values = (tokens[...].astype(jnp.float32) + attended).astype(jnp.bfloat16)
    residual[...] = values
    quartet = jnp.concatenate(
        [project_with(picked(places[part], OWN), values) for part in range(4)], axis=1
    )
    merged[...] = layer_norm(quartet, gain[...]).astype(jnp.bfloat16)


def coarse_kernel(
    order, coarse, gain, row_order, first, second, third, fourth, out, pieces, arrived
):
    copies = [
        pltpu.make_async_copy(piece, pieces.at[place], arrived.at[place])
        for place, piece in enumerate((first, second, third, fourth))
    ]
    for copy in copies:
        copy.start()
    normed = layer_norm(coarse[...].astype(jnp.float32), gain[...]).astype(jnp.bfloat16)
    normed = project_with(normed, row_order[...]).astype(jnp.bfloat16)
    lower = lax.broadcasted_iota(jnp.int32, (1, 2 * HEAD), 1) < HEAD
    for place, copy in enumerate(copies):
        copy.wait()
        packed = jnp.zeros((normed.shape[0], 384), jnp.float32)
        for part in range(4):
            packed += project_with(
                normed[:, 256 * part : 256 * (part + 1)],
                pieces[place, :, 384 * part : 384 * (part + 1)],
            )
        packed = packed.astype(jnp.bfloat16)
        mixed = pair_mix(packed[:, :128], packed[:, 128:256], packed[:, 256:], lower, None)
        out[order[place]] = mixed.astype(jnp.bfloat16)


def final_kernel(core, expanded, first_sum, second_sum, gain, residual, places, out):
    half = jnp.where(core[0] == 0, residual[:, :256], residual[:, 256:]).astype(jnp.float32)
    own_gain = jnp.where(core[0] == 0, gain[:, :256], gain[:, 256:])
    total = half
    for part in range(4):
        average = first_sum[:, part : part + 1] / 512
        spread = second_sum[:, part : part + 1] / 512 - average * average
        values = expanded[:, 256 * part : 256 * (part + 1)] - average
        values = values * lax.rsqrt(spread + EPSILON) * own_gain
        high = values.astype(jnp.bfloat16)
        low = (values - high.astype(jnp.float32)).astype(jnp.bfloat16)
        back = spread_out(places[part], OWN)
        total = total + (project_with(back, high) + project_with(back, low))
    out[...] = total.astype(jnp.bfloat16)


def sent_to_all(block, axes):
    peers = lax.axis_size(axes)
    copies = jnp.broadcast_to(block[None], (peers,) + block.shape)
    return lax.all_to_all(copies, axes, split_axis=0, concat_axis=0, tiled=True)


def depth_pair(block):
    other = lax.ppermute(block, "za", [(0, 1), (1, 0)])
    upper = lax.axis_index("za") == 1
    return jnp.stack([jnp.where(upper, other, block), jnp.where(upper, block, other)])


def from_others(block, axis):
    return [block] + [
        lax.ppermute(block, axis, [((i + by) % 4, i) for i in range(4)]) for by in (1, 2, 3)
    ]


def lat_shift(value, by):
    perm = [(i, (i + by) % 32) for i in range(32)]
    return lax.ppermute(value, ("za", "zq", "x"), perm)


def lon_shift(value, by):
    perm = [(i, (i + by) % 8) for i in range(8)]
    return lax.ppermute(value, ("y", "zh"), perm)


def body(
    fine_tokens,
    attn_gain,
    fine_qkv,
    fine_proj,
    merge_gain,
    merge_weight,
    coarse_gain,
    coarse_qkv,
    coarse_proj,
    split_weight,
    split_gain,
):
    lat_total = ROWS * 32
    row_first = lax.axis_index(("za", "zq", "x")) * ROWS
    core = lax.axis_index("core").astype(jnp.int32)[None]
    x_place, y_place = lax.axis_index("x"), lax.axis_index("y")
    flat_tokens = fine_tokens.reshape(OWN, 512)

    early, late_shard = call(
        pack_kernel,
        (shape(8, 3200), shape(88, 1536)),
        (
            y_place.astype(jnp.int32)[None],
            fine_qkv,
            fine_proj.T,
            merge_weight,
            coarse_qkv,
            coarse_proj.T,
            split_weight,
        ),
        scalars=1,
    )
    early, late_shard, first_tokens = lax.optimization_barrier((early, late_shard, flat_tokens))
    normed, first_cols, last_cols = call(
        norm_kernel,
        (shape(OWN, 512), shape(SIDE, 256), shape(SIDE, 256)),
        (core, first_tokens, attn_gain[None], FIRST_COLS, LAST_COLS),
        scalars=1,
    )
    late = lax.all_gather(late_shard, "x", axis=0, tiled=False)
    late = late[:, :32].reshape(128, 1536)
    depth = sent_to_all(depth_pair(early), "zq")
    east = lon_shift(first_cols, -1)
    west = lon_shift(last_cols, 1)
    depth, late, east, west = lax.optimization_barrier((depth, late, east, west))
    late = lax.all_gather(late, ("za", "zq"), axis=0, tiled=True)
    merge_side = sent_to_all(depth[..., :1664], "y")
    qkv_quad = jnp.stack(from_others(depth[..., 1664:], "x")).reshape(256, 1536)
    merge_side, qkv_quad, east, west = lax.optimization_barrier(
        (merge_side, qkv_quad, east, west)
    )
    qkv_pieces = from_others(qkv_quad, "y")
    both_all = sent_to_all(merge_side, "x")
    first_rows, last_rows = call(
        ends_kernel,
        (shape(ENDS, 256), shape(ENDS, 256)),
        (core, normed, west, east, FIRST_ROWS, LAST_ROWS),
        scalars=1,
    )
    below = lat_shift(first_rows, -1)
    above = lat_shift(last_rows, 1)
    rims = jnp.concatenate([west, east, above, below], axis=0)
    rims = lax.all_gather(rims, "core", axis=1, tiled=True)
    windows = call(
        window_kernel,
        shape(9, WINDOW, 512),
        (normed, rims, WINDOWS[:, :, None]),
        grid=(9,),
        in_specs=[
            pl.BlockSpec((OWN, 512), lambda i: (0, 0)),
            pl.BlockSpec((RIMS, 512), lambda i: (0, 0)),
            pl.BlockSpec((1, WINDOW, 1), lambda i: (i, 0, 0)),
        ],
        out_specs=pl.BlockSpec((1, WINDOW, 512), lambda i: (i, 0, 0)),
    )
    global_rows = row_first - RIM_ROWS + jnp.arange(ROWS + 2 * RIM_ROWS, dtype=jnp.int32)
    labels = seam_labels((global_rows + lat_total) % lat_total, lat_total, RIM_ROWS)
    labels = labels.reshape(3, 1, WIN_LAT, 1)
    labels = jnp.broadcast_to(labels, (3, LEVELS, WIN_LAT, WIN_LON)).reshape(3, WINDOW)
    bias = jnp.where(labels[:, :, None] == labels[:, None, :], 0.0, -1e30).astype(jnp.float32)

    first_all = both_all[..., :640].reshape(4, 2, 2, 4, 2, 8, 640)
    left_weight, right_weight = (
        first_all[:, :, part].transpose(3, 2, 0, 1, 4, 5).reshape(512, 640) for part in range(2)
    )

    constant = lambda i: (0, 0)
    window_out = call(
        fine_kernel,
        shape(OWN, 256),
        (windows, left_weight, right_weight, bias, WINDOWS[:, None, :]),
        grid=(9,),
        in_specs=[
            pl.BlockSpec((1, WINDOW, 512), lambda i: (i, 0, 0)),
            pl.BlockSpec((512, 640), constant),
            pl.BlockSpec((512, 640), constant),
            pl.BlockSpec((1, WINDOW, WINDOW), lambda i: (i // 3, 0, 0)),
            pl.BlockSpec((1, 1, WINDOW), lambda i: (i, 0, 0)),
        ],
        out_specs=pl.BlockSpec((OWN, 256), constant),
        scratch_shapes=[pltpu.VMEM((OWN, 256), jnp.float32)],
    )
    all_heads = lax.all_gather(window_out, "core", axis=1, tiled=True)
    residual, merged_in = call(
        merge_kernel,
        (shape(OWN, 512), shape(COARSE, 2048)),
        (all_heads, right_weight, flat_tokens, merge_gain[None], QUARTETS[:, :, None]),
    )
    merge_all = jnp.stack([both_all[..., 640:1152], both_all[..., 1152:]], axis=4)
    merge_all = merge_all.transpose(3, 2, 0, 1, 4, 5, 6).reshape(2048, 512)
    coarse_half = project_with(merged_in, merge_all).astype(jnp.bfloat16)
    coarse_full = lax.all_gather(coarse_half, "core", axis=1, tiled=True)

    place = jnp.arange(1024, dtype=jnp.int32)
    feature = place // 8 % 2 * 512 + place // 16 % 4 * 128 + (place // 64 + x_place) % 4 * 32
    feature = feature + place // 256 * 8 + place % 8
    row_order = (place[:, None] == feature[None, :]).astype(jnp.bfloat16)
    qkv_pieces, late = lax.optimization_barrier((qkv_pieces, late))
    order = (y_place + jnp.arange(4, dtype=jnp.int32)) % 4
    coarse_mixed = call(
        coarse_kernel,
        shape(4, COARSE, 128),
        (order, coarse_full, coarse_gain[None], row_order, *qkv_pieces),
        in_specs=[pl.BlockSpec(memory_space=pltpu.SMEM)]
        + [pl.BlockSpec(memory_space=pltpu.VMEM)] * 3
        + [pl.BlockSpec(memory_space=pl.ANY)] * 4,
        scratch_shapes=[
            pltpu.VMEM((4, 256, 1536), jnp.bfloat16),
            pltpu.SemaphoreType.DMA((4,)),
        ],
    )
    coarse_mixed = coarse_mixed.transpose(1, 0, 2).reshape(COARSE, 512)
    partial_value = project_with_transposed(coarse_mixed, late[:, 1024:]).astype(jnp.bfloat16)
    both = lax.all_gather(partial_value, "core", axis=0, tiled=False).astype(jnp.float32)
    coarse_out = (coarse_full.astype(jnp.float32) + (both[0] + both[1])).astype(jnp.bfloat16)
    expanded = project_with(coarse_out, late[:, :1024])
    parts = expanded.reshape(COARSE, 4, 256)
    first_sum, second_sum = lax.psum(
        (jnp.sum(parts, axis=-1), jnp.sum(parts * parts, axis=-1)), "core"
    )
    restored = call(
        final_kernel,
        shape(OWN, 256),
        (
            core,
            expanded,
            first_sum,
            second_sum,
            split_gain[None],
            residual,
            QUARTETS[:, None, :],
        ),
        scalars=1,
    )
    return restored.reshape(LEVELS, ROWS, COLS, 256)


def solution(mesh):
    finer = Mesh(
        mesh.devices.reshape(2, 4, 4, 4, 2, 2), ("za", "zq", "x", "y", "zh", "core")
    )
    lat, lon, tp = ("za", "zq", "x"), ("y", "zh"), "core"
    in_specs = (
        P(None, lat, lon, None),
        P(),
        P(lat, None, tp),
        P(None, lat),
        P(),
        P(lat, tp),
        P(),
        P(lat, None, tp),
        P(tp, lat),
        P(lat, None, tp),
        P(),
    )
    out_specs = P(None, lat, lon, tp)
    return jax.shard_map(body, mesh=finer, in_specs=in_specs, out_specs=out_specs, check_vma=False)
```

```python
import jax
import jax.numpy as jnp
import numpy as np
from jax import lax
from jax.experimental import pallas as pl
from jax.experimental.pallas import tpu as pltpu
from jax.sharding import Mesh, PartitionSpec as P

HEAD = 64
WIN_LAT = 6
WIN_LON = 12


EPSILON = 1e-05

LEVELS, ROWS, COLS = 2, 12, 24
RIM_ROWS, RIM_COLS = WIN_LAT // 2, WIN_LON // 2
OWN = LEVELS * ROWS * COLS
SIDE = LEVELS * ROWS * RIM_COLS
ENDS = LEVELS * RIM_ROWS * (COLS + 2 * RIM_COLS)
RIMS = 2 * SIDE + 2 * ENDS
WINDOW = LEVELS * WIN_LAT * WIN_LON
COARSE = OWN // 4


def wide_places():
    wide = np.zeros((LEVELS, ROWS + 2 * RIM_ROWS, COLS + 2 * RIM_COLS), np.int32)
    rows, cols = slice(RIM_ROWS, RIM_ROWS + ROWS), slice(RIM_COLS, RIM_COLS + COLS)
    start = 0
    for part in (
        wide[:, rows, cols],
        wide[:, rows, :RIM_COLS],
        wide[:, rows, RIM_COLS + COLS :],
        wide[:, :RIM_ROWS],
        wide[:, RIM_ROWS + ROWS :],
    ):
        part[...] = start + np.arange(part.size).reshape(part.shape)
        start += part.size
    return wide


WIDE = wide_places()
OWN_ROWS = slice(RIM_ROWS, RIM_ROWS + ROWS)
FIRST_COLS = WIDE[:, OWN_ROWS, RIM_COLS : 2 * RIM_COLS].reshape(-1, 1)
LAST_COLS = WIDE[:, OWN_ROWS, COLS : COLS + RIM_COLS].reshape(-1, 1)
FIRST_ROWS = WIDE[:, RIM_ROWS : 2 * RIM_ROWS].reshape(-1, 1)
LAST_ROWS = WIDE[:, ROWS : ROWS + RIM_ROWS].reshape(-1, 1)
WINDOWS = (
    WIDE.reshape(LEVELS, 3, WIN_LAT, 3, WIN_LON).transpose(1, 3, 0, 2, 4).reshape(9, WINDOW)
)
QUARTETS = (
    np.arange(OWN, dtype=np.int32)
    .reshape(LEVELS, ROWS // 2, 2, COLS // 2, 2)
    .transpose(2, 4, 0, 1, 3)
    .reshape(4, COARSE)
)


def layer_norm(values, gain_row):
    average = jnp.mean(values, axis=-1, keepdims=True)
    centred = values - average
    spread = jnp.mean(centred * centred, axis=-1, keepdims=True)
    return centred * lax.rsqrt(spread + EPSILON) * gain_row


def seam_labels(global_rows, lat_total, rim_rows):
    return jnp.where(
        global_rows >= lat_total - rim_rows, 1, jnp.where(global_rows < rim_rows, 2, 0)
    ).astype(jnp.int32)


def project_with(left_side, fragment):
    return jnp.dot(left_side, fragment, preferred_element_type=jnp.float32)


def project_with_transposed(left_side, fragment):
    return lax.dot_general(
        left_side, fragment, (((1,), (1,)), ((), ())), preferred_element_type=jnp.float32
    )


def picked(column, count):
    places = lax.broadcasted_iota(jnp.int32, (column.shape[0], count), 1)
    return (places == column).astype(jnp.bfloat16)


def spread_out(row, count):
    places = lax.broadcasted_iota(jnp.int32, (count, row.shape[1]), 0)
    return (places == row).astype(jnp.bfloat16)


def pair_mix(query, keys, values, lower, bias):
    mixed = []
    for keep in (lower, ~lower):
        kept = query * jnp.where(keep, HEAD**-0.5, 0.0).astype(jnp.bfloat16)
        scores = project_with_transposed(kept, keys)
        if bias is not None:
            scores = scores + bias
        weights = jnp.exp(scores - jnp.max(scores, axis=-1, keepdims=True))
        total = jnp.sum(weights, axis=-1, keepdims=True)
        mixed.append(project_with(weights.astype(jnp.bfloat16), values) / total)
    return jnp.where(lower, *mixed)


def call(kernel, out_shape, operands, scalars=0, limit=24, flops=10**8, **options):
    whole = pl.BlockSpec(memory_space=pltpu.VMEM)
    options.setdefault(
        "in_specs",
        [pl.BlockSpec(memory_space=pltpu.SMEM)] * scalars + [whole] * (len(operands) - scalars),
    )
    options.setdefault("out_specs", jax.tree.map(lambda _: whole, out_shape))
    return pl.pallas_call(
        kernel,
        out_shape=out_shape,
        compiler_params=pltpu.CompilerParams(vmem_limit_bytes=limit * 2**20),
        cost_estimate=pl.CostEstimate(flops=flops, bytes_accessed=2**20, transcendentals=0),
        **options,
    )(*operands)


def shape(*sizes, dtype=jnp.bfloat16):
    return jax.ShapeDtypeStruct(sizes, dtype)


def pack_kernel(place, fine_qkv, fine_proj, merge, coarse_qkv, coarse_proj, split, early, late):
    y = place[0]
    wide = jnp.concatenate(
        [fine_qkv[part].astype(jnp.float32) for part in range(3)]
        + [fine_proj[...].astype(jnp.float32)],
        axis=1,
    )
    half = jnp.where(y >= 2, wide[8:], wide[:8])
    odd = (y == 1) | (y == 3)
    early[:, :640] = jnp.where(odd, half[:, 640:], half[:, :640]).astype(jnp.bfloat16)
    rows = merge[pl.ds(pl.multiple_of(y * 16, 16), 16), :].astype(jnp.float32)
    early[:, 640:1152] = rows[:8].astype(jnp.bfloat16)
    early[:, 1152:1664] = rows[8:].astype(jnp.bfloat16)
    for part in range(3):
        cols = coarse_qkv[part, :, pl.ds(pl.multiple_of(y * 128, 128), 128)].astype(jnp.float32)
        for block in range(4):
            start = 1664 + 384 * block + 128 * part
            early[:, start : start + 128] = cols[8 * block : 8 * block + 8].astype(jnp.bfloat16)
    late[...] = jnp.zeros_like(late)
    for part in range(4):
        late[:32, 256 * part : 256 * (part + 1)] = split[:, part, :]
    late[:32, 1024:] = coarse_proj[...]


def norm_kernel(core, tokens, gain, first_place, last_place, normed, first, last):
    values = layer_norm(tokens[...].astype(jnp.float32), gain[...]).astype(jnp.bfloat16)
    normed[...] = values
    half = jnp.where(core[0] == 0, values[:, :256], values[:, 256:])
    first[...] = project_with(picked(first_place[...], OWN), half).astype(jnp.bfloat16)
    last[...] = project_with(picked(last_place[...], OWN), half).astype(jnp.bfloat16)


def ends_kernel(core, normed, west, east, first_place, last_place, first, last):
    half = jnp.where(core[0] == 0, normed[:, :256], normed[:, 256:])
    for place, out in ((first_place, first), (last_place, last)):
        pick = picked(place[...], OWN + 2 * SIDE)
        rows = project_with(pick[:, :OWN], half)
        rows += project_with(pick[:, OWN : OWN + SIDE], west[...])
        rows += project_with(pick[:, OWN + SIDE :], east[...])
        out[...] = rows.astype(jnp.bfloat16)


def window_kernel(normed, rims, column, out):
    pick = picked(column[0], OWN + RIMS)
    rows = project_with(pick[:, :OWN], normed[...]) + project_with(pick[:, OWN:], rims[...])
    out[0] = rows.astype(jnp.bfloat16)


def fine_kernel(windows, left_weight, right_weight, bias, row, out, total):
    window = pl.program_id(0)
    tokens = windows[0]
    left = project_with(tokens, left_weight[...]).astype(jnp.bfloat16)
    right = project_with(tokens, right_weight[:, :128]).astype(jnp.bfloat16)
    lower = lax.broadcasted_iota(jnp.int32, (1, 2 * HEAD), 1) < HEAD
    values = (left[:, 512:640], right)
    mixed = [
        pair_mix(
            left[:, 128 * pair : 128 * (pair + 1)],
            left[:, 256 + 128 * pair : 256 + 128 * (pair + 1)],
            values[pair],
            lower,
            bias[0],
        ).astype(jnp.bfloat16)
        for pair in range(2)
    ]

    @pl.when(window == 0)
    def _():
        total[...] = jnp.zeros_like(total)

    total[...] += project_with(spread_out(row[0], OWN), jnp.concatenate(mixed, axis=1))

    @pl.when(window == 8)
    def _():
        out[...] = total[...].astype(jnp.bfloat16)


def merge_kernel(heads, weight, tokens, gain, places, residual, merged):
    attended = project_with_transposed(heads[...], weight[:, 128:])
    values = (tokens[...].astype(jnp.float32) + attended).astype(jnp.bfloat16)
    residual[...] = values
    quartet = jnp.concatenate(
        [project_with(picked(places[part], OWN), values) for part in range(4)], axis=1
    )
    merged[...] = layer_norm(quartet, gain[...]).astype(jnp.bfloat16)


def coarse_kernel(
    order, coarse, gain, row_order, first, second, third, fourth, out, pieces, arrived
):
    copies = [
        [
            pltpu.make_async_copy(
                quad.at[place], pieces.at[place, 64 * x : 64 * (x + 1)], arrived.at[place, x]
            )
            for x, quad in enumerate((first, second, third, fourth))
        ]
        for place in range(4)
    ]
    for piece in copies:
        for copy in piece:
            copy.start()
    normed = layer_norm(coarse[...].astype(jnp.float32), gain[...]).astype(jnp.bfloat16)
    normed = project_with(normed, row_order[...]).astype(jnp.bfloat16)
    lower = lax.broadcasted_iota(jnp.int32, (1, 2 * HEAD), 1) < HEAD
    for place, piece in enumerate(copies):
        for copy in piece:
            copy.wait()
        packed = jnp.zeros((normed.shape[0], 384), jnp.float32)
        for part in range(4):
            packed += project_with(
                normed[:, 256 * part : 256 * (part + 1)],
                pieces[place, :, 384 * part : 384 * (part + 1)],
            )
        packed = packed.astype(jnp.bfloat16)
        mixed = pair_mix(packed[:, :128], packed[:, 128:256], packed[:, 256:], lower, None)
        out[order[place]] = mixed.astype(jnp.bfloat16)


def final_kernel(core, expanded, sums, gain, residual, places, out):
    half = jnp.where(core[0] == 0, residual[:, :256], residual[:, 256:]).astype(jnp.float32)
    own_gain = jnp.where(core[0] == 0, gain[:, :256], gain[:, 256:])
    both = sums[:COARSE] + sums[COARSE:]
    total = half
    for part in range(4):
        average = both[:, part : part + 1] / 512
        spread = both[:, 4 + part : 5 + part] / 512 - average * average
        values = expanded[:, 256 * part : 256 * (part + 1)] - average
        values = values * lax.rsqrt(spread + EPSILON) * own_gain
        high = values.astype(jnp.bfloat16)
        low = (values - high.astype(jnp.float32)).astype(jnp.bfloat16)
        back = spread_out(places[part], OWN)
        total = total + (project_with(back, high) + project_with(back, low))
    out[...] = total.astype(jnp.bfloat16)


def sent_to_all(block, axes):
    peers = lax.axis_size(axes)
    copies = jnp.broadcast_to(block[None], (peers,) + block.shape)
    return lax.all_to_all(copies, axes, split_axis=0, concat_axis=0, tiled=True)


def depth_pair(block):
    other = lax.ppermute(block, "za", [(0, 1), (1, 0)])
    upper = lax.axis_index("za") == 1
    return jnp.stack([jnp.where(upper, other, block), jnp.where(upper, block, other)])


def from_others(block, axis):
    return [block] + [
        lax.ppermute(block, axis, [((i + by) % 4, i) for i in range(4)]) for by in (1, 2, 3)
    ]


def lat_shift(value, by):
    perm = [(i, (i + by) % 32) for i in range(32)]
    return lax.ppermute(value, ("za", "zq", "x"), perm)


def body(
    fine_tokens,
    attn_gain,
    fine_qkv,
    fine_proj,
    merge_gain,
    merge_weight,
    coarse_gain,
    coarse_qkv,
    coarse_proj,
    split_weight,
    split_gain,
):
    lat_total = ROWS * 32
    row_first = lax.axis_index(("za", "zq", "x")) * ROWS
    core = lax.axis_index("core").astype(jnp.int32)[None]
    x_place, y_place = lax.axis_index("x"), lax.axis_index("y")
    flat_tokens = fine_tokens.reshape(OWN, 512)

    early, late_shard = call(
        pack_kernel,
        (shape(8, 3200), shape(88, 1536)),
        (
            y_place.astype(jnp.int32)[None],
            fine_qkv.transpose(1, 0, 2),
            fine_proj.T,
            merge_weight,
            coarse_qkv.transpose(1, 0, 2),
            coarse_proj.T,
            split_weight,
        ),
        scalars=1,
    )
    early, late_shard, first_tokens = lax.optimization_barrier((early, late_shard, flat_tokens))
    normed, first_cols, last_cols = call(
        norm_kernel,
        (shape(OWN, 512), shape(SIDE, 256), shape(SIDE, 256)),
        (core, first_tokens, attn_gain[None], FIRST_COLS, LAST_COLS),
        scalars=1,
    )
    late = lax.all_gather(late_shard, "x", axis=0, tiled=False)
    late = late[:, :32].reshape(128, 1536)
    depth = sent_to_all(depth_pair(early), "zq")
    even = lax.axis_index("zh") == 0
    same_row = lax.ppermute(jnp.where(even, last_cols, first_cols), "zh", [(0, 1), (1, 0)])
    perm = [(2 * i + 1, (2 * i + 2) % 8) for i in range(4)]
    perm += [(there, here) for here, there in perm]
    next_row = lax.ppermute(jnp.where(even, first_cols, last_cols), ("y", "zh"), perm)
    depth, late, same_row = lax.optimization_barrier((depth, late, same_row))
    late = lax.all_gather(late, ("za", "zq"), axis=0, tiled=True)
    merge_side = sent_to_all(depth[..., :1664], "x")
    qkv_quad = jnp.stack(from_others(depth[..., 1664:], "y")).reshape(4, 64, 1536)
    merge_side, qkv_quad, same_row, next_row = lax.optimization_barrier(
        (merge_side, qkv_quad, same_row, next_row)
    )
    east = jnp.where(even, same_row, next_row)
    west = jnp.where(even, next_row, same_row)
    qkv_pieces = from_others(qkv_quad, "x")
    both_all = sent_to_all(merge_side, "y")
    first_rows, last_rows = call(
        ends_kernel,
        (shape(ENDS, 256), shape(ENDS, 256)),
        (core, normed, west, east, FIRST_ROWS, LAST_ROWS),
        scalars=1,
    )
    below = lat_shift(first_rows, -1)
    above = lat_shift(last_rows, 1)
    rims = jnp.concatenate([west, east, above, below], axis=0)
    rims = lax.all_gather(rims, "core", axis=1, tiled=True)
    windows = call(
        window_kernel,
        shape(9, WINDOW, 512),
        (normed, rims, WINDOWS[:, :, None]),
        grid=(9,),
        in_specs=[
            pl.BlockSpec((OWN, 512), lambda i: (0, 0)),
            pl.BlockSpec((RIMS, 512), lambda i: (0, 0)),
            pl.BlockSpec((1, WINDOW, 1), lambda i: (i, 0, 0)),
        ],
        out_specs=pl.BlockSpec((1, WINDOW, 512), lambda i: (i, 0, 0)),
    )
    global_rows = row_first - RIM_ROWS + jnp.arange(ROWS + 2 * RIM_ROWS, dtype=jnp.int32)
    labels = seam_labels((global_rows + lat_total) % lat_total, lat_total, RIM_ROWS)
    labels = labels.reshape(3, 1, WIN_LAT, 1)
    labels = jnp.broadcast_to(labels, (3, LEVELS, WIN_LAT, WIN_LON)).reshape(3, WINDOW)
    bias = jnp.where(labels[:, :, None] == labels[:, None, :], 0.0, -1e30).astype(jnp.float32)

    first_all = both_all[..., :640].reshape(2, 2, 4, 4, 2, 8, 640)
    left_weight, right_weight = (
        first_all[:, part].transpose(3, 2, 1, 0, 4, 5).reshape(512, 640) for part in range(2)
    )

    constant = lambda i: (0, 0)
    window_out = call(
        fine_kernel,
        shape(OWN, 256),
        (windows, left_weight, right_weight, bias, WINDOWS[:, None, :]),
        grid=(9,),
        in_specs=[
            pl.BlockSpec((1, WINDOW, 512), lambda i: (i, 0, 0)),
            pl.BlockSpec((512, 640), constant),
            pl.BlockSpec((512, 640), constant),
            pl.BlockSpec((1, WINDOW, WINDOW), lambda i: (i // 3, 0, 0)),
            pl.BlockSpec((1, 1, WINDOW), lambda i: (i, 0, 0)),
        ],
        out_specs=pl.BlockSpec((OWN, 256), constant),
        scratch_shapes=[pltpu.VMEM((OWN, 256), jnp.float32)],
    )
    all_heads = lax.all_gather(window_out, "core", axis=1, tiled=True)
    residual, merged_in = call(
        merge_kernel,
        (shape(OWN, 512), shape(COARSE, 2048)),
        (all_heads, right_weight, flat_tokens, merge_gain[None], QUARTETS[:, :, None]),
    )
    merge_all = jnp.stack([both_all[..., 640:1152], both_all[..., 1152:]], axis=4)
    merge_all = merge_all.transpose(3, 2, 1, 0, 4, 5, 6).reshape(2048, 512)
    coarse_half = project_with(merged_in, merge_all).astype(jnp.bfloat16)
    coarse_full = lax.all_gather(coarse_half, "core", axis=1, tiled=True)

    place = jnp.arange(1024, dtype=jnp.int32)
    feature = place // 8 % 2 * 512 + place // 16 % 4 * 128 + (place // 64 + x_place) % 4 * 32
    feature = feature + place // 256 * 8 + place % 8
    row_order = (place[:, None] == feature[None, :]).astype(jnp.bfloat16)
    qkv_pieces, late = lax.optimization_barrier((qkv_pieces, late))
    order = (y_place + jnp.arange(4, dtype=jnp.int32)) % 4
    coarse_mixed = call(
        coarse_kernel,
        shape(4, COARSE, 128),
        (order, coarse_full, coarse_gain[None], row_order, *qkv_pieces),
        in_specs=[pl.BlockSpec(memory_space=pltpu.SMEM)]
        + [pl.BlockSpec(memory_space=pltpu.VMEM)] * 3
        + [pl.BlockSpec(memory_space=pl.ANY)] * 4,
        scratch_shapes=[
            pltpu.VMEM((4, 256, 1536), jnp.bfloat16),
            pltpu.SemaphoreType.DMA((4, 4)),
        ],
    )
    coarse_mixed = coarse_mixed.transpose(1, 0, 2).reshape(COARSE, 512)
    partial_value = project_with_transposed(coarse_mixed, late[:, 1024:]).astype(jnp.bfloat16)
    both = lax.all_gather(partial_value, "core", axis=0, tiled=False).astype(jnp.float32)
    coarse_out = (coarse_full.astype(jnp.float32) + (both[0] + both[1])).astype(jnp.bfloat16)
    expanded = project_with(coarse_out, late[:, :1024])
    parts = expanded.reshape(COARSE, 4, 256)
    sums = jnp.concatenate([jnp.sum(parts, axis=-1), jnp.sum(parts * parts, axis=-1)], axis=1)
    sums = lax.all_gather(sums, "core", axis=0, tiled=True)
    restored = call(
        final_kernel,
        shape(OWN, 256),
        (
            core,
            expanded,
            sums,
            split_gain[None],
            residual,
            QUARTETS[:, None, :],
        ),
        scalars=1,
    )
    return restored.reshape(LEVELS, ROWS, COLS, 256)


def solution(mesh):
    finer = Mesh(
        mesh.devices.reshape(2, 4, 4, 4, 2, 2), ("za", "zq", "x", "y", "zh", "core")
    )
    lat, lon, tp = ("za", "zq", "x"), ("y", "zh"), "core"
    in_specs = (
        P(None, lat, lon, None),
        P(),
        P(lat, None, tp),
        P(None, lat),
        P(),
        P(lat, tp),
        P(),
        P(lat, None, tp),
        P(tp, lat),
        P(lat, None, tp),
        P(),
    )
    out_specs = P(None, lat, lon, tp)
    return jax.shard_map(body, mesh=finer, in_specs=in_specs, out_specs=out_specs, check_vma=False)
```

```python
import jax
import jax.numpy as jnp
import numpy as np
from jax import lax
from jax.experimental import pallas as pl
from jax.experimental.pallas import tpu as pltpu
from jax.sharding import Mesh, PartitionSpec as P

HEAD = 64
WIN_LAT = 6
WIN_LON = 12


EPSILON = 1e-05

LEVELS, ROWS, COLS = 2, 12, 24
RIM_ROWS, RIM_COLS = WIN_LAT // 2, WIN_LON // 2
OWN = LEVELS * ROWS * COLS
SIDE = LEVELS * ROWS * RIM_COLS
ENDS = LEVELS * RIM_ROWS * (COLS + 2 * RIM_COLS)
RIMS = 2 * SIDE + 2 * ENDS
WINDOW = LEVELS * WIN_LAT * WIN_LON
COARSE = OWN // 4


def wide_places():
    wide = np.zeros((LEVELS, ROWS + 2 * RIM_ROWS, COLS + 2 * RIM_COLS), np.int32)
    rows, cols = slice(RIM_ROWS, RIM_ROWS + ROWS), slice(RIM_COLS, RIM_COLS + COLS)
    start = 0
    for part in (
        wide[:, rows, cols],
        wide[:, rows, :RIM_COLS],
        wide[:, rows, RIM_COLS + COLS :],
        wide[:, :RIM_ROWS],
        wide[:, RIM_ROWS + ROWS :],
    ):
        part[...] = start + np.arange(part.size).reshape(part.shape)
        start += part.size
    return wide


WIDE = wide_places()
OWN_ROWS = slice(RIM_ROWS, RIM_ROWS + ROWS)
FIRST_COLS = WIDE[:, OWN_ROWS, RIM_COLS : 2 * RIM_COLS].reshape(-1, 1)
LAST_COLS = WIDE[:, OWN_ROWS, COLS : COLS + RIM_COLS].reshape(-1, 1)
FIRST_ROWS = WIDE[:, RIM_ROWS : 2 * RIM_ROWS].reshape(-1, 1)
LAST_ROWS = WIDE[:, ROWS : ROWS + RIM_ROWS].reshape(-1, 1)
WINDOWS = (
    WIDE.reshape(LEVELS, 3, WIN_LAT, 3, WIN_LON).transpose(1, 3, 0, 2, 4).reshape(9, WINDOW)
)
QUARTETS = (
    np.arange(OWN, dtype=np.int32)
    .reshape(LEVELS, ROWS // 2, 2, COLS // 2, 2)
    .transpose(2, 4, 0, 1, 3)
    .reshape(4, COARSE)
)


def layer_norm(values, gain_row):
    average = jnp.mean(values, axis=-1, keepdims=True)
    centred = values - average
    spread = jnp.mean(centred * centred, axis=-1, keepdims=True)
    return centred * lax.rsqrt(spread + EPSILON) * gain_row


def seam_labels(global_rows, lat_total, rim_rows):
    return jnp.where(
        global_rows >= lat_total - rim_rows, 1, jnp.where(global_rows < rim_rows, 2, 0)
    ).astype(jnp.int32)


def project_with(left_side, fragment):
    return jnp.dot(left_side, fragment, preferred_element_type=jnp.float32)


def project_with_transposed(left_side, fragment):
    return lax.dot_general(
        left_side, fragment, (((1,), (1,)), ((), ())), preferred_element_type=jnp.float32
    )


def picked(column, count):
    places = lax.broadcasted_iota(jnp.int32, (column.shape[0], count), 1)
    return (places == column).astype(jnp.bfloat16)


def spread_out(row, count):
    places = lax.broadcasted_iota(jnp.int32, (count, row.shape[1]), 0)
    return (places == row).astype(jnp.bfloat16)


def pair_mix(query, keys, values, lower, bias):
    mixed = []
    for keep in (lower, ~lower):
        kept = query * jnp.where(keep, HEAD**-0.5, 0.0).astype(jnp.bfloat16)
        scores = project_with_transposed(kept, keys)
        if bias is not None:
            scores = scores + bias
        weights = jnp.exp(scores - jnp.max(scores, axis=-1, keepdims=True))
        total = jnp.sum(weights, axis=-1, keepdims=True)
        mixed.append(project_with(weights.astype(jnp.bfloat16), values) / total)
    return jnp.where(lower, *mixed)


def call(kernel, out_shape, operands, scalars=0, limit=24, flops=10**8, **options):
    whole = pl.BlockSpec(memory_space=pltpu.VMEM)
    options.setdefault(
        "in_specs",
        [pl.BlockSpec(memory_space=pltpu.SMEM)] * scalars + [whole] * (len(operands) - scalars),
    )
    options.setdefault("out_specs", jax.tree.map(lambda _: whole, out_shape))
    return pl.pallas_call(
        kernel,
        out_shape=out_shape,
        compiler_params=pltpu.CompilerParams(vmem_limit_bytes=limit * 2**20),
        cost_estimate=pl.CostEstimate(flops=flops, bytes_accessed=2**20, transcendentals=0),
        **options,
    )(*operands)


def shape(*sizes, dtype=jnp.bfloat16):
    return jax.ShapeDtypeStruct(sizes, dtype)


def pack_kernel(place, fine_qkv, fine_proj, merge, coarse_qkv, coarse_proj, split, early, late):
    y = place[0]
    wide = jnp.concatenate(
        [fine_qkv[part].astype(jnp.float32) for part in range(3)]
        + [fine_proj[...].astype(jnp.float32)],
        axis=1,
    )
    half = jnp.where(y >= 2, wide[8:], wide[:8])
    odd = (y == 1) | (y == 3)
    early[:, :640] = jnp.where(odd, half[:, 640:], half[:, :640]).astype(jnp.bfloat16)
    rows = merge[pl.ds(pl.multiple_of(y * 16, 16), 16), :].astype(jnp.float32)
    early[:, 640:1152] = rows[:8].astype(jnp.bfloat16)
    early[:, 1152:1664] = rows[8:].astype(jnp.bfloat16)
    for part in range(3):
        cols = coarse_qkv[part, :, pl.ds(pl.multiple_of(y * 128, 128), 128)].astype(jnp.float32)
        for block in range(4):
            start = 1664 + 384 * block + 128 * part
            early[:, start : start + 128] = cols[8 * block : 8 * block + 8].astype(jnp.bfloat16)
    late[...] = jnp.zeros_like(late)
    for part in range(4):
        late[:32, 256 * part : 256 * (part + 1)] = split[:, part, :]
    late[:32, 1024:] = coarse_proj[...]


def norm_kernel(core, tokens, gain, first_place, last_place, normed, first, last):
    values = layer_norm(tokens[...].astype(jnp.float32), gain[...]).astype(jnp.bfloat16)
    normed[...] = values
    half = jnp.where(core[0] == 0, values[:, :256], values[:, 256:])
    first[...] = project_with(picked(first_place[...], OWN), half).astype(jnp.bfloat16)
    last[...] = project_with(picked(last_place[...], OWN), half).astype(jnp.bfloat16)


def ends_kernel(core, normed, west, east, first_place, last_place, first, last):
    half = jnp.where(core[0] == 0, normed[:, :256], normed[:, 256:])
    for place, out in ((first_place, first), (last_place, last)):
        pick = picked(place[...], OWN + 2 * SIDE)
        rows = project_with(pick[:, :OWN], half)
        rows += project_with(pick[:, OWN : OWN + SIDE], west[...])
        rows += project_with(pick[:, OWN + SIDE :], east[...])
        out[...] = rows.astype(jnp.bfloat16)


def window_kernel(normed, rims, column, out):
    pick = picked(column[0], OWN + RIMS)
    rows = project_with(pick[:, :OWN], normed[...]) + project_with(pick[:, OWN:], rims[...])
    out[0] = rows.astype(jnp.bfloat16)


def fine_kernel(windows, left_weight, right_weight, bias, row, out, total):
    window = pl.program_id(0)
    tokens = windows[0]
    left = project_with(tokens, left_weight[...]).astype(jnp.bfloat16)
    right = project_with(tokens, right_weight[:, :128]).astype(jnp.bfloat16)
    lower = lax.broadcasted_iota(jnp.int32, (1, 2 * HEAD), 1) < HEAD
    values = (left[:, 512:640], right)
    mixed = [
        pair_mix(
            left[:, 128 * pair : 128 * (pair + 1)],
            left[:, 256 + 128 * pair : 256 + 128 * (pair + 1)],
            values[pair],
            lower,
            bias[0],
        ).astype(jnp.bfloat16)
        for pair in range(2)
    ]

    @pl.when(window == 0)
    def _():
        total[...] = jnp.zeros_like(total)

    total[...] += project_with(spread_out(row[0], OWN), jnp.concatenate(mixed, axis=1))

    @pl.when(window == 8)
    def _():
        out[...] = total[...].astype(jnp.bfloat16)


def merge_kernel(heads, weight, tokens, gain, places, residual, merged):
    attended = project_with_transposed(heads[...], weight[:, 128:])
    values = (tokens[...].astype(jnp.float32) + attended).astype(jnp.bfloat16)
    residual[...] = values
    quartet = jnp.concatenate(
        [project_with(picked(places[part], OWN), values) for part in range(4)], axis=1
    )
    merged[...] = layer_norm(quartet, gain[...]).astype(jnp.bfloat16)


def coarse_kernel(
    order, coarse, gain, row_order, first, second, third, fourth, out, pieces, arrived
):
    copies = [
        [
            pltpu.make_async_copy(
                quad.at[place], pieces.at[place, 64 * x : 64 * (x + 1)], arrived.at[place, x]
            )
            for x, quad in enumerate((first, second, third, fourth))
        ]
        for place in range(4)
    ]
    for piece in copies:
        for copy in piece:
            copy.start()
    normed = layer_norm(coarse[...].astype(jnp.float32), gain[...]).astype(jnp.bfloat16)
    normed = project_with(normed, row_order[...]).astype(jnp.bfloat16)
    lower = lax.broadcasted_iota(jnp.int32, (1, 2 * HEAD), 1) < HEAD
    for place, piece in enumerate(copies):
        for copy in piece:
            copy.wait()
        packed = jnp.zeros((normed.shape[0], 384), jnp.float32)
        for part in range(4):
            packed += project_with(
                normed[:, 256 * part : 256 * (part + 1)],
                pieces[place, :, 384 * part : 384 * (part + 1)],
            )
        packed = packed.astype(jnp.bfloat16)
        mixed = pair_mix(packed[:, :128], packed[:, 128:256], packed[:, 256:], lower, None)
        out[order[place]] = mixed.astype(jnp.bfloat16)


def final_kernel(core, expanded, sums, gain, residual, places, out):
    half = jnp.where(core[0] == 0, residual[:, :256], residual[:, 256:]).astype(jnp.float32)
    own_gain = jnp.where(core[0] == 0, gain[:, :256], gain[:, 256:])
    both = sums[:COARSE] + sums[COARSE:]
    total = half
    for part in range(4):
        average = both[:, part : part + 1] / 512
        spread = both[:, 4 + part : 5 + part] / 512 - average * average
        values = expanded[:, 256 * part : 256 * (part + 1)] - average
        values = values * lax.rsqrt(spread + EPSILON) * own_gain
        high = values.astype(jnp.bfloat16)
        low = (values - high.astype(jnp.float32)).astype(jnp.bfloat16)
        back = spread_out(places[part], OWN)
        total = total + (project_with(back, high) + project_with(back, low))
    out[...] = total.astype(jnp.bfloat16)


def sent_to_all(block, axes):
    peers = lax.axis_size(axes)
    copies = jnp.broadcast_to(block[None], (peers,) + block.shape)
    return lax.all_to_all(copies, axes, split_axis=0, concat_axis=0, tiled=True)


def depth_pair(block):
    other = lax.ppermute(block, "za", [(0, 1), (1, 0)])
    upper = lax.axis_index("za") == 1
    return jnp.stack([jnp.where(upper, other, block), jnp.where(upper, block, other)])


def from_others(block, axis):
    return [block] + [
        lax.ppermute(block, axis, [((i + by) % 4, i) for i in range(4)]) for by in (1, 2, 3)
    ]


def lat_shift(value, by):
    perm = [(i, (i + by) % 32) for i in range(32)]
    return lax.ppermute(value, ("za", "zq", "x"), perm)


def body(
    fine_tokens,
    attn_gain,
    fine_qkv,
    fine_proj,
    merge_gain,
    merge_weight,
    coarse_gain,
    coarse_qkv,
    coarse_proj,
    split_weight,
    split_gain,
):
    lat_total = ROWS * 32
    row_first = lax.axis_index(("za", "zq", "x")) * ROWS
    core = lax.axis_index("core").astype(jnp.int32)[None]
    x_place, y_place = lax.axis_index("x"), lax.axis_index("y")
    flat_tokens = fine_tokens.reshape(OWN, 512)

    early, late_shard = call(
        pack_kernel,
        (shape(8, 3200), shape(88, 1536)),
        (
            y_place.astype(jnp.int32)[None],
            fine_qkv.transpose(1, 0, 2),
            fine_proj.T,
            merge_weight,
            coarse_qkv.transpose(1, 0, 2),
            coarse_proj.T,
            split_weight,
        ),
        scalars=1,
    )
    early, late_shard, first_tokens = lax.optimization_barrier((early, late_shard, flat_tokens))
    normed, first_cols, last_cols = call(
        norm_kernel,
        (shape(OWN, 512), shape(SIDE, 256), shape(SIDE, 256)),
        (core, first_tokens, attn_gain[None], FIRST_COLS, LAST_COLS),
        scalars=1,
    )
    late = lax.all_gather(late_shard, "x", axis=0, tiled=False)
    late = late[:, :32].reshape(128, 1536)
    depth = sent_to_all(depth_pair(early), "zq")
    even = lax.axis_index("zh") == 0
    same_row = lax.ppermute(jnp.where(even, last_cols, first_cols), "zh", [(0, 1), (1, 0)])
    perm = [(2 * i + 1, (2 * i + 2) % 8) for i in range(4)]
    perm += [(there, here) for here, there in perm]
    next_row = lax.ppermute(jnp.where(even, first_cols, last_cols), ("y", "zh"), perm)
    depth, same_row = lax.optimization_barrier((depth, same_row))
    merge_side = sent_to_all(depth[..., :1664], "x")
    depth, late = lax.optimization_barrier((depth, late))
    late = lax.all_gather(late, ("za", "zq"), axis=0, tiled=True)
    qkv_quad = jnp.stack(from_others(depth[..., 1664:], "y")).reshape(4, 64, 1536)
    merge_side, qkv_quad = lax.optimization_barrier((merge_side, qkv_quad))
    east = jnp.where(even, same_row, next_row)
    west = jnp.where(even, next_row, same_row)
    qkv_pieces = from_others(qkv_quad, "x")
    both_all = sent_to_all(merge_side, "y")
    first_rows, last_rows = call(
        ends_kernel,
        (shape(ENDS, 256), shape(ENDS, 256)),
        (core, normed, west, east, FIRST_ROWS, LAST_ROWS),
        scalars=1,
    )
    below = lat_shift(first_rows, -1)
    above = lat_shift(last_rows, 1)
    rims = jnp.concatenate([west, east, above, below], axis=0)
    rims = lax.all_gather(rims, "core", axis=1, tiled=True)
    windows = call(
        window_kernel,
        shape(9, WINDOW, 512),
        (normed, rims, WINDOWS[:, :, None]),
        grid=(9,),
        in_specs=[
            pl.BlockSpec((OWN, 512), lambda i: (0, 0)),
            pl.BlockSpec((RIMS, 512), lambda i: (0, 0)),
            pl.BlockSpec((1, WINDOW, 1), lambda i: (i, 0, 0)),
        ],
        out_specs=pl.BlockSpec((1, WINDOW, 512), lambda i: (i, 0, 0)),
    )
    global_rows = row_first - RIM_ROWS + jnp.arange(ROWS + 2 * RIM_ROWS, dtype=jnp.int32)
    labels = seam_labels((global_rows + lat_total) % lat_total, lat_total, RIM_ROWS)
    labels = labels.reshape(3, 1, WIN_LAT, 1)
    labels = jnp.broadcast_to(labels, (3, LEVELS, WIN_LAT, WIN_LON)).reshape(3, WINDOW)
    bias = jnp.where(labels[:, :, None] == labels[:, None, :], 0.0, -1e30).astype(jnp.float32)

    first_all = both_all[..., :640].reshape(2, 2, 4, 4, 2, 8, 640)
    left_weight, right_weight = (
        first_all[:, part].transpose(3, 2, 1, 0, 4, 5).reshape(512, 640) for part in range(2)
    )

    constant = lambda i: (0, 0)
    window_out = call(
        fine_kernel,
        shape(OWN, 256),
        (windows, left_weight, right_weight, bias, WINDOWS[:, None, :]),
        grid=(9,),
        in_specs=[
            pl.BlockSpec((1, WINDOW, 512), lambda i: (i, 0, 0)),
            pl.BlockSpec((512, 640), constant),
            pl.BlockSpec((512, 640), constant),
            pl.BlockSpec((1, WINDOW, WINDOW), lambda i: (i // 3, 0, 0)),
            pl.BlockSpec((1, 1, WINDOW), lambda i: (i, 0, 0)),
        ],
        out_specs=pl.BlockSpec((OWN, 256), constant),
        scratch_shapes=[pltpu.VMEM((OWN, 256), jnp.float32)],
    )
    all_heads = lax.all_gather(window_out, "core", axis=1, tiled=True)
    all_heads, qkv_pieces = lax.optimization_barrier((all_heads, qkv_pieces))
    residual, merged_in = call(
        merge_kernel,
        (shape(OWN, 512), shape(COARSE, 2048)),
        (all_heads, right_weight, flat_tokens, merge_gain[None], QUARTETS[:, :, None]),
    )
    merge_all = jnp.stack([both_all[..., 640:1152], both_all[..., 1152:]], axis=4)
    merge_all = merge_all.transpose(3, 2, 1, 0, 4, 5, 6).reshape(2048, 512)
    coarse_half = project_with(merged_in, merge_all).astype(jnp.bfloat16)
    coarse_full = lax.all_gather(coarse_half, "core", axis=1, tiled=True)

    place = jnp.arange(1024, dtype=jnp.int32)
    feature = place // 8 % 2 * 512 + place // 16 % 4 * 128 + (place // 64 + x_place) % 4 * 32
    feature = feature + place // 256 * 8 + place % 8
    row_order = (place[:, None] == feature[None, :]).astype(jnp.bfloat16)
    qkv_pieces, late = lax.optimization_barrier((qkv_pieces, late))
    order = (y_place + jnp.arange(4, dtype=jnp.int32)) % 4
    coarse_mixed = call(
        coarse_kernel,
        shape(4, COARSE, 128),
        (order, coarse_full, coarse_gain[None], row_order, *qkv_pieces),
        in_specs=[pl.BlockSpec(memory_space=pltpu.SMEM)]
        + [pl.BlockSpec(memory_space=pltpu.VMEM)] * 3
        + [pl.BlockSpec(memory_space=pl.ANY)] * 4,
        scratch_shapes=[
            pltpu.VMEM((4, 256, 1536), jnp.bfloat16),
            pltpu.SemaphoreType.DMA((4, 4)),
        ],
    )
    coarse_mixed = coarse_mixed.transpose(1, 0, 2).reshape(COARSE, 512)
    partial_value = project_with_transposed(coarse_mixed, late[:, 1024:]).astype(jnp.bfloat16)
    both = lax.all_gather(partial_value, "core", axis=0, tiled=False).astype(jnp.float32)
    coarse_out = (coarse_full.astype(jnp.float32) + (both[0] + both[1])).astype(jnp.bfloat16)
    expanded = project_with(coarse_out, late[:, :1024])
    parts = expanded.reshape(COARSE, 4, 256)
    sums = jnp.concatenate([jnp.sum(parts, axis=-1), jnp.sum(parts * parts, axis=-1)], axis=1)
    sums = lax.all_gather(sums, "core", axis=0, tiled=True)
    restored = call(
        final_kernel,
        shape(OWN, 256),
        (
            core,
            expanded,
            sums,
            split_gain[None],
            residual,
            QUARTETS[:, None, :],
        ),
        scalars=1,
    )
    return restored.reshape(LEVELS, ROWS, COLS, 256)


def solution(mesh):
    finer = Mesh(
        mesh.devices.reshape(2, 4, 4, 4, 2, 2), ("za", "zq", "x", "y", "zh", "core")
    )
    lat, lon, tp = ("za", "zq", "x"), ("y", "zh"), "core"
    in_specs = (
        P(None, lat, lon, None),
        P(),
        P(lat, None, tp),
        P(None, lat),
        P(),
        P(lat, tp),
        P(),
        P(lat, None, tp),
        P(tp, lat),
        P(lat, None, tp),
        P(),
    )
    out_specs = P(None, lat, lon, tp)
    return jax.shard_map(body, mesh=finer, in_specs=in_specs, out_specs=out_specs, check_vma=False)
```

```python
import jax
import jax.numpy as jnp
import numpy as np
from jax import lax
from jax.experimental import pallas as pl
from jax.experimental.pallas import tpu as pltpu
from jax.sharding import Mesh, PartitionSpec as P

HEAD = 64
WIN_LAT = 6
WIN_LON = 12


EPSILON = 1e-05

LEVELS, ROWS, COLS = 2, 12, 24
RIM_ROWS, RIM_COLS = WIN_LAT // 2, WIN_LON // 2
OWN = LEVELS * ROWS * COLS
SIDE = LEVELS * ROWS * RIM_COLS
ENDS = LEVELS * RIM_ROWS * (COLS + 2 * RIM_COLS)
RIMS = 2 * SIDE + 2 * ENDS
WINDOW = LEVELS * WIN_LAT * WIN_LON
COARSE = OWN // 4


def wide_places():
    wide = np.zeros((LEVELS, ROWS + 2 * RIM_ROWS, COLS + 2 * RIM_COLS), np.int32)
    rows, cols = slice(RIM_ROWS, RIM_ROWS + ROWS), slice(RIM_COLS, RIM_COLS + COLS)
    start = 0
    for part in (
        wide[:, rows, cols],
        wide[:, rows, :RIM_COLS],
        wide[:, rows, RIM_COLS + COLS :],
        wide[:, :RIM_ROWS],
        wide[:, RIM_ROWS + ROWS :],
    ):
        part[...] = start + np.arange(part.size).reshape(part.shape)
        start += part.size
    return wide


WIDE = wide_places()
OWN_ROWS = slice(RIM_ROWS, RIM_ROWS + ROWS)
FIRST_COLS = WIDE[:, OWN_ROWS, RIM_COLS : 2 * RIM_COLS].reshape(-1, 1)
LAST_COLS = WIDE[:, OWN_ROWS, COLS : COLS + RIM_COLS].reshape(-1, 1)
FIRST_ROWS = WIDE[:, RIM_ROWS : 2 * RIM_ROWS].reshape(-1, 1)
LAST_ROWS = WIDE[:, ROWS : ROWS + RIM_ROWS].reshape(-1, 1)
WINDOWS = (
    WIDE.reshape(LEVELS, 3, WIN_LAT, 3, WIN_LON).transpose(1, 3, 0, 2, 4).reshape(9, WINDOW)
)
QUARTETS = (
    np.arange(OWN, dtype=np.int32)
    .reshape(LEVELS, ROWS // 2, 2, COLS // 2, 2)
    .transpose(2, 4, 0, 1, 3)
    .reshape(4, COARSE)
)


def layer_norm(values, gain_row):
    average = jnp.mean(values, axis=-1, keepdims=True)
    centred = values - average
    spread = jnp.mean(centred * centred, axis=-1, keepdims=True)
    return centred * lax.rsqrt(spread + EPSILON) * gain_row


def seam_labels(global_rows, lat_total, rim_rows):
    return jnp.where(
        global_rows >= lat_total - rim_rows, 1, jnp.where(global_rows < rim_rows, 2, 0)
    ).astype(jnp.int32)


def project_with(left_side, fragment):
    return jnp.dot(left_side, fragment, preferred_element_type=jnp.float32)


def project_with_transposed(left_side, fragment):
    return lax.dot_general(
        left_side, fragment, (((1,), (1,)), ((), ())), preferred_element_type=jnp.float32
    )


def picked(column, count):
    places = lax.broadcasted_iota(jnp.int32, (column.shape[0], count), 1)
    return (places == column).astype(jnp.bfloat16)


def spread_out(row, count):
    places = lax.broadcasted_iota(jnp.int32, (count, row.shape[1]), 0)
    return (places == row).astype(jnp.bfloat16)


def pair_mix(query, keys, values, lower, bias):
    mixed = []
    for keep in (lower, ~lower):
        kept = query * jnp.where(keep, HEAD**-0.5, 0.0).astype(jnp.bfloat16)
        scores = project_with_transposed(kept, keys)
        if bias is not None:
            scores = scores + bias
        weights = jnp.exp(scores - jnp.max(scores, axis=-1, keepdims=True))
        total = jnp.sum(weights, axis=-1, keepdims=True)
        mixed.append(project_with(weights.astype(jnp.bfloat16), values) / total)
    return jnp.where(lower, *mixed)


def call(kernel, out_shape, operands, scalars=0, limit=24, flops=10**8, **options):
    whole = pl.BlockSpec(memory_space=pltpu.VMEM)
    options.setdefault(
        "in_specs",
        [pl.BlockSpec(memory_space=pltpu.SMEM)] * scalars + [whole] * (len(operands) - scalars),
    )
    options.setdefault("out_specs", jax.tree.map(lambda _: whole, out_shape))
    return pl.pallas_call(
        kernel,
        out_shape=out_shape,
        compiler_params=pltpu.CompilerParams(vmem_limit_bytes=limit * 2**20),
        cost_estimate=pl.CostEstimate(flops=flops, bytes_accessed=2**20, transcendentals=0),
        **options,
    )(*operands)


def shape(*sizes, dtype=jnp.bfloat16):
    return jax.ShapeDtypeStruct(sizes, dtype)


def pack_kernel(place, fine_qkv, fine_proj, merge, coarse_qkv, coarse_proj, split, early, late):
    y = place[0]
    wide = jnp.concatenate(
        [fine_qkv[part].astype(jnp.float32) for part in range(3)]
        + [fine_proj[...].astype(jnp.float32)],
        axis=1,
    )
    half = jnp.where(y >= 2, wide[8:], wide[:8])
    odd = (y == 1) | (y == 3)
    early[:, :640] = jnp.where(odd, half[:, 640:], half[:, :640]).astype(jnp.bfloat16)
    rows = merge[pl.ds(pl.multiple_of(y * 16, 16), 16), :].astype(jnp.float32)
    early[:, 640:1152] = rows[:8].astype(jnp.bfloat16)
    early[:, 1152:1664] = rows[8:].astype(jnp.bfloat16)
    for part in range(3):
        cols = coarse_qkv[part, :, pl.ds(pl.multiple_of(y * 128, 128), 128)].astype(jnp.float32)
        for block in range(4):
            start = 1664 + 384 * block + 128 * part
            early[:, start : start + 128] = cols[8 * block : 8 * block + 8].astype(jnp.bfloat16)
    late[...] = jnp.zeros_like(late)
    for part in range(4):
        late[:32, 256 * part : 256 * (part + 1)] = split[:, part, :]
    late[:32, 1024:] = coarse_proj[...]


def norm_kernel(core, tokens, gain, first_place, last_place, normed, first, last):
    values = layer_norm(tokens[...].astype(jnp.float32), gain[...]).astype(jnp.bfloat16)
    normed[...] = values
    half = jnp.where(core[0] == 0, values[:, :256], values[:, 256:])
    first[...] = project_with(picked(first_place[...], OWN), half).astype(jnp.bfloat16)
    last[...] = project_with(picked(last_place[...], OWN), half).astype(jnp.bfloat16)


def ends_kernel(core, normed, west, east, first_place, last_place, first, last):
    half = jnp.where(core[0] == 0, normed[:, :256], normed[:, 256:])
    for place, out in ((first_place, first), (last_place, last)):
        pick = picked(place[...], OWN + 2 * SIDE)
        rows = project_with(pick[:, :OWN], half)
        rows += project_with(pick[:, OWN : OWN + SIDE], west[...])
        rows += project_with(pick[:, OWN + SIDE :], east[...])
        out[...] = rows.astype(jnp.bfloat16)


def window_kernel(normed, rims, column, out):
    pick = picked(column[0], OWN + RIMS)
    rows = project_with(pick[:, :OWN], normed[...]) + project_with(pick[:, OWN:], rims[...])
    out[0] = rows.astype(jnp.bfloat16)


def fine_kernel(windows, left_weight, right_weight, bias, row, out, total):
    window = pl.program_id(0)
    tokens = windows[0]
    left = project_with(tokens, left_weight[...]).astype(jnp.bfloat16)
    right = project_with(tokens, right_weight[:, :128]).astype(jnp.bfloat16)
    lower = lax.broadcasted_iota(jnp.int32, (1, 2 * HEAD), 1) < HEAD
    values = (left[:, 512:640], right)
    mixed = [
        pair_mix(
            left[:, 128 * pair : 128 * (pair + 1)],
            left[:, 256 + 128 * pair : 256 + 128 * (pair + 1)],
            values[pair],
            lower,
            bias[0],
        ).astype(jnp.bfloat16)
        for pair in range(2)
    ]

    @pl.when(window == 0)
    def _():
        total[...] = jnp.zeros_like(total)

    total[...] += project_with(spread_out(row[0], OWN), jnp.concatenate(mixed, axis=1))

    @pl.when(window == 8)
    def _():
        out[...] = total[...].astype(jnp.bfloat16)


def merge_kernel(heads, weight, tokens, gain, places, residual, merged):
    attended = project_with_transposed(heads[...], weight[:, 128:])
    values = (tokens[...].astype(jnp.float32) + attended).astype(jnp.bfloat16)
    residual[...] = values
    quartet = jnp.concatenate(
        [project_with(picked(places[part], OWN), values) for part in range(4)], axis=1
    )
    merged[...] = layer_norm(quartet, gain[...]).astype(jnp.bfloat16)


def coarse_kernel(
    order, coarse, gain, row_order, first, second, third, fourth, out, pieces, arrived
):
    copies = [
        [
            pltpu.make_async_copy(
                quad.at[place], pieces.at[place, 64 * x : 64 * (x + 1)], arrived.at[place, x]
            )
            for x, quad in enumerate((first, second, third, fourth))
        ]
        for place in range(4)
    ]
    for piece in copies:
        for copy in piece:
            copy.start()
    normed = layer_norm(coarse[...].astype(jnp.float32), gain[...]).astype(jnp.bfloat16)
    normed = project_with(normed, row_order[...]).astype(jnp.bfloat16)
    lower = lax.broadcasted_iota(jnp.int32, (1, 2 * HEAD), 1) < HEAD
    for place, piece in enumerate(copies):
        for copy in piece:
            copy.wait()
        packed = jnp.zeros((normed.shape[0], 384), jnp.float32)
        for part in range(4):
            packed += project_with(
                normed[:, 256 * part : 256 * (part + 1)],
                pieces[place, :, 384 * part : 384 * (part + 1)],
            )
        packed = packed.astype(jnp.bfloat16)
        mixed = pair_mix(packed[:, :128], packed[:, 128:256], packed[:, 256:], lower, None)
        out[order[place]] = mixed.astype(jnp.bfloat16)


def final_kernel(core, expanded, sums, gain, residual, places, out):
    half = jnp.where(core[0] == 0, residual[:, :256], residual[:, 256:]).astype(jnp.float32)
    own_gain = jnp.where(core[0] == 0, gain[:, :256], gain[:, 256:])
    both = sums[:COARSE] + sums[COARSE:]
    total = half
    for part in range(4):
        average = both[:, part : part + 1] / 512
        spread = both[:, 4 + part : 5 + part] / 512 - average * average
        values = expanded[:, 256 * part : 256 * (part + 1)] - average
        values = values * lax.rsqrt(spread + EPSILON) * own_gain
        high = values.astype(jnp.bfloat16)
        low = (values - high.astype(jnp.float32)).astype(jnp.bfloat16)
        back = spread_out(places[part], OWN)
        total = total + (project_with(back, high) + project_with(back, low))
    out[...] = total.astype(jnp.bfloat16)


def sent_to_all(block, axes):
    peers = lax.axis_size(axes)
    copies = jnp.broadcast_to(block[None], (peers,) + block.shape)
    return lax.all_to_all(copies, axes, split_axis=0, concat_axis=0, tiled=True)


def depth_pair(block):
    other = lax.ppermute(block, "za", [(0, 1), (1, 0)])
    upper = lax.axis_index("za") == 1
    return jnp.stack([jnp.where(upper, other, block), jnp.where(upper, block, other)])


def from_others(block, axis):
    return [block] + [
        lax.ppermute(block, axis, [((i + by) % 4, i) for i in range(4)]) for by in (1, 2, 3)
    ]


def lat_shift(value, by):
    perm = [(i, (i + by) % 32) for i in range(32)]
    return lax.ppermute(value, ("za", "zq", "x"), perm)


def body(
    fine_tokens,
    attn_gain,
    fine_qkv,
    fine_proj,
    merge_gain,
    merge_weight,
    coarse_gain,
    coarse_qkv,
    coarse_proj,
    split_weight,
    split_gain,
):
    lat_total = ROWS * 32
    row_first = lax.axis_index(("za", "zq", "x")) * ROWS
    core = lax.axis_index("core").astype(jnp.int32)[None]
    x_place, y_place = lax.axis_index("x"), lax.axis_index("y")
    flat_tokens = fine_tokens.reshape(OWN, 512)

    early, late_shard = call(
        pack_kernel,
        (shape(8, 3200), shape(88, 1536)),
        (
            y_place.astype(jnp.int32)[None],
            fine_qkv.transpose(1, 0, 2),
            fine_proj.T,
            merge_weight,
            coarse_qkv.transpose(1, 0, 2),
            coarse_proj.T,
            split_weight,
        ),
        scalars=1,
    )
    early, late_shard, first_tokens = lax.optimization_barrier((early, late_shard, flat_tokens))
    normed, first_cols, last_cols = call(
        norm_kernel,
        (shape(OWN, 512), shape(SIDE, 256), shape(SIDE, 256)),
        (core, first_tokens, attn_gain[None], FIRST_COLS, LAST_COLS),
        scalars=1,
    )
    late = lax.all_gather(late_shard, "x", axis=0, tiled=False)
    late = late[:, :32].reshape(128, 1536)
    depth = sent_to_all(depth_pair(early), "zq")
    even = lax.axis_index("zh") == 0
    same_row = lax.ppermute(jnp.where(even, last_cols, first_cols), "zh", [(0, 1), (1, 0)])
    perm = [(2 * i + 1, (2 * i + 2) % 8) for i in range(4)]
    perm += [(there, here) for here, there in perm]
    next_row = lax.ppermute(jnp.where(even, first_cols, last_cols), ("y", "zh"), perm)
    depth, same_row = lax.optimization_barrier((depth, same_row))
    merge_side = sent_to_all(depth[..., :1664], "x")
    depth, late = lax.optimization_barrier((depth, late))
    late = lax.all_gather(late, ("za", "zq"), axis=0, tiled=True)
    qkv_quad = jnp.stack(from_others(depth[..., 1664:], "y")).reshape(4, 64, 1536)
    merge_side, qkv_quad, same_row, next_row = lax.optimization_barrier(
        (merge_side, qkv_quad, same_row, next_row)
    )
    east = jnp.where(even, same_row, next_row)
    west = jnp.where(even, next_row, same_row)
    qkv_pieces = from_others(qkv_quad, "x")
    both_all = sent_to_all(merge_side, "y")
    first_rows, last_rows = call(
        ends_kernel,
        (shape(ENDS, 256), shape(ENDS, 256)),
        (core, normed, west, east, FIRST_ROWS, LAST_ROWS),
        scalars=1,
    )
    below = lat_shift(first_rows, -1)
    above = lat_shift(last_rows, 1)
    rims = jnp.concatenate([west, east, above, below], axis=0)
    rims = lax.all_gather(rims, "core", axis=1, tiled=True)
    windows = call(
        window_kernel,
        shape(9, WINDOW, 512),
        (normed, rims, WINDOWS[:, :, None]),
        grid=(9,),
        in_specs=[
            pl.BlockSpec((OWN, 512), lambda i: (0, 0)),
            pl.BlockSpec((RIMS, 512), lambda i: (0, 0)),
            pl.BlockSpec((1, WINDOW, 1), lambda i: (i, 0, 0)),
        ],
        out_specs=pl.BlockSpec((1, WINDOW, 512), lambda i: (i, 0, 0)),
    )
    global_rows = row_first - RIM_ROWS + jnp.arange(ROWS + 2 * RIM_ROWS, dtype=jnp.int32)
    labels = seam_labels((global_rows + lat_total) % lat_total, lat_total, RIM_ROWS)
    labels = labels.reshape(3, 1, WIN_LAT, 1)
    labels = jnp.broadcast_to(labels, (3, LEVELS, WIN_LAT, WIN_LON)).reshape(3, WINDOW)
    bias = jnp.where(labels[:, :, None] == labels[:, None, :], 0.0, -1e30).astype(jnp.float32)

    first_all = both_all[..., :640].reshape(2, 2, 4, 4, 2, 8, 640)
    left_weight, right_weight = (
        first_all[:, part].transpose(3, 2, 1, 0, 4, 5).reshape(512, 640) for part in range(2)
    )

    constant = lambda i: (0, 0)
    window_out = call(
        fine_kernel,
        shape(OWN, 256),
        (windows, left_weight, right_weight, bias, WINDOWS[:, None, :]),
        grid=(9,),
        in_specs=[
            pl.BlockSpec((1, WINDOW, 512), lambda i: (i, 0, 0)),
            pl.BlockSpec((512, 640), constant),
            pl.BlockSpec((512, 640), constant),
            pl.BlockSpec((1, WINDOW, WINDOW), lambda i: (i // 3, 0, 0)),
            pl.BlockSpec((1, 1, WINDOW), lambda i: (i, 0, 0)),
        ],
        out_specs=pl.BlockSpec((OWN, 256), constant),
        scratch_shapes=[pltpu.VMEM((OWN, 256), jnp.float32)],
    )
    all_heads = lax.all_gather(window_out, "core", axis=1, tiled=True)
    residual, merged_in = call(
        merge_kernel,
        (shape(OWN, 512), shape(COARSE, 2048)),
        (all_heads, right_weight, flat_tokens, merge_gain[None], QUARTETS[:, :, None]),
    )
    merge_all = jnp.stack([both_all[..., 640:1152], both_all[..., 1152:]], axis=4)
    merge_all = merge_all.transpose(3, 2, 1, 0, 4, 5, 6).reshape(2048, 512)
    coarse_half = project_with(merged_in, merge_all).astype(jnp.bfloat16)
    coarse_full = lax.all_gather(coarse_half, "core", axis=1, tiled=True)

    place = jnp.arange(1024, dtype=jnp.int32)
    feature = place // 8 % 2 * 512 + place // 16 % 4 * 128 + (place // 64 + x_place) % 4 * 32
    feature = feature + place // 256 * 8 + place % 8
    row_order = (place[:, None] == feature[None, :]).astype(jnp.bfloat16)
    qkv_pieces, late = lax.optimization_barrier((qkv_pieces, late))
    order = (y_place + jnp.arange(4, dtype=jnp.int32)) % 4
    coarse_mixed = call(
        coarse_kernel,
        shape(4, COARSE, 128),
        (order, coarse_full, coarse_gain[None], row_order, *qkv_pieces),
        in_specs=[pl.BlockSpec(memory_space=pltpu.SMEM)]
        + [pl.BlockSpec(memory_space=pltpu.VMEM)] * 3
        + [pl.BlockSpec(memory_space=pl.ANY)] * 4,
        scratch_shapes=[
            pltpu.VMEM((4, 256, 1536), jnp.bfloat16),
            pltpu.SemaphoreType.DMA((4, 4)),
        ],
    )
    coarse_mixed = coarse_mixed.transpose(1, 0, 2).reshape(COARSE, 512)
    partial_value = project_with_transposed(coarse_mixed, late[:, 1024:]).astype(jnp.bfloat16)
    both = lax.all_gather(partial_value, "core", axis=0, tiled=False).astype(jnp.float32)
    coarse_out = (coarse_full.astype(jnp.float32) + (both[0] + both[1])).astype(jnp.bfloat16)
    expanded = project_with(coarse_out, late[:, :1024])
    parts = expanded.reshape(COARSE, 4, 256)
    sums = jnp.concatenate([jnp.sum(parts, axis=-1), jnp.sum(parts * parts, axis=-1)], axis=1)
    sums = lax.all_gather(sums, "core", axis=0, tiled=True)
    restored = call(
        final_kernel,
        shape(OWN, 256),
        (
            core,
            expanded,
            sums,
            split_gain[None],
            residual,
            QUARTETS[:, None, :],
        ),
        scalars=1,
    )
    return restored.reshape(LEVELS, ROWS, COLS, 256)


def solution(mesh):
    finer = Mesh(
        mesh.devices.reshape(2, 4, 4, 4, 2, 2), ("za", "zq", "x", "y", "zh", "core")
    )
    lat, lon, tp = ("za", "zq", "x"), ("y", "zh"), "core"
    in_specs = (
        P(None, lat, lon, None),
        P(),
        P(lat, None, tp),
        P(None, lat),
        P(),
        P(lat, tp),
        P(),
        P(lat, None, tp),
        P(tp, lat),
        P(lat, None, tp),
        P(),
    )
    out_specs = P(None, lat, lon, tp)
    return jax.shard_map(body, mesh=finer, in_specs=in_specs, out_specs=out_specs, check_vma=False)
```
